128 devices in a mesh: section: 2 (over core), expert: 32 (over z, x, y_hi), dp: 2 (over y_lo).
Axes of the slice: x: 4, y: 4 (y_hi: 2, y_lo: 2; y = y_hi * 2 + y_lo), z: 4, core: 2. Of those that a mesh axis runs over, the one named last changes fastest.
Arguments:
- images_in: bfloat16 [2, 64, 197, 384], P(None, ('expert', 'dp')), may hold values from -6 to 6
- cotangent: bfloat16 [2, 64, 197, 384], P(None, ('expert', 'dp')), may hold values from -6 to 6
- gain_one: float32 [2, 384], P('section'), may hold values from 0.1 to 1.9
- w_qkv: bfloat16 [2, 384, 1152], P('section'), may hold values from -0.3125 to 0.3125
- w_out: bfloat16 [2, 384, 384], P('section'), may hold values from -1.75 to 1.75
- gain_two: float32 [2, 384], P('section'), may hold values from 0.1 to 1.9
- w_router: float32 [2, 384, 32], P('section'), may hold values from -0.21875 to 0.21875
- w_in: bfloat16 [2, 32, 384, 1536], P('section', 'expert'), may hold values from -0.3125 to 0.3125
- w_back: bfloat16 [2, 32, 1536, 384], P('section', 'expert'), may hold values from -2 to 2
- routes: int32 [2, 2, 64, 197, 2], P('section', None, ('expert', 'dp')), may hold values from 0 to 31, all different within a row; in each aligned block of 197 rows (0 to 196, 197 to 393, ..., all dimensions but the last counted through in order) at most 19 rows name the same one
- keep: int32 [2, 2, 64, 197, 2], P('section', None, ('expert', 'dp')), may hold values 0 or 1
Outputs:
- activations: bfloat16 [2, 2, 64, 197, 384], P('section', None, ('expert', 'dp'))
- input_grad: float32 [2, 2, 64, 197, 384], P('section', None, ('expert', 'dp'))
- d_gain_one: float32 [2, 384], P('section')
- d_w_qkv: float32 [2, 384, 1152], P('section')
- d_w_out: float32 [2, 384, 384], P('section')
- d_gain_two: float32 [2, 384], P('section')
- d_w_router: float32 [2, 384, 32], P('section')
- d_w_in: float32 [2, 32, 384, 1536], P('section', 'expert')
- d_w_back: float32 [2, 32, 1536, 384], P('section', 'expert')
The draws below stay inside these ranges and needn't reach their ends.
Inputs may be any that keep to these rules, and one draw needn't show every extreme that they name: `routes`: A token's two choices are different experts. In the tokens of one device for one block and micro-batch (1 images), no expert is chosen more than 19 times.
All inputs are finite; a program needn't handle non-finite values. No bound on the sum of `keep` on one device may be relied on, other than what follows from the above.
Results may differ from the reference program's by a relative error of at most 0.02.
Values may be sent and summed in bfloat16 or wider, within the bound.
A program may use at most 128 MiB of HBM per device.

```python
import math
import jax
import jax.numpy as jnp
import numpy as np
from jax import lax

D = 384
HEADS = 6
HEAD = 64
FF = 1536
SEQ = 197
IMG_DEV = 1
MICRO = 2
SECTIONS = 2
EXPERTS = 32
IMAGES = 64
CAP = 19
N_EXPERT = 32
N_DP = 2


def set_ends(array, key, smallest, largest):
    spot = [jax.random.randint(jax.random.fold_in(key, axis), (), 0, length) for axis, length in enumerate(array.shape)]
    longest = array.shape.index(max(array.shape))
    beside = spot[:longest] + [(spot[longest] + 1) % array.shape[longest]] + spot[longest + 1:]
    return array.at[tuple(spot)].set(smallest).at[tuple(beside)].set(largest)


def steps_of(rng, shape, shards, smallest, largest):
    def one(position, parts):
        heights = jax.random.uniform(jax.random.fold_in(jax.random.fold_in(rng, 6), position), (parts,), jnp.float32, smallest / len(shards), largest / len(shards))
        return jnp.repeat(jnp.exp(heights), shape[position] // parts).reshape((-1,) + (1,) * (len(shape) - position - 1))

    factor_of = one(*shards[0])
    for cut in shards[1:]:
        factor_of = factor_of * one(*cut)
    return factor_of


def shared_out(rng, own, number, rows, number_of, top, bound, lean):
    sequence = jax.random.permutation(rng, number_of)
    crowded, ordinary = portions_of(number_of, rows * top, bound, lean, True), portions_of(number_of, rows * top, bound, lean, False)
    places = jnp.arange(number_of)

    def named(tallies, rotation):
        used = int((tallies > 0).sum())
        fixed = max(1, used // 4)
        moved = fixed + (places - fixed + rotation * (used - fixed)) % max(1, number_of - fixed)
        return jnp.zeros((number_of,), jnp.int32).at[sequence[jnp.where(places < fixed, places, moved)]].set(jnp.asarray(tallies, jnp.int32))

    tallies = jnp.where(number % 4 == 0, named(crowded, number // 4), named(ordinary, number - number // 4 - 1))
    mixed = jax.random.permutation(jax.random.fold_in(own, 3), number_of)
    donor, taker = mixed[0:number_of // 2 * 2:2], mixed[1:number_of // 2 * 2:2]
    margin = jnp.minimum(tallies[donor] - 1, bound - tallies[taker]) // 2
    margin = jnp.where((donor == sequence[0]) | (taker == sequence[0]) | (tallies[taker] == 0), 0, jnp.maximum(margin, 0))
    moved = jax.random.randint(jax.random.fold_in(own, 4), (number_of // 2,), 0, 1 << 20) % (margin + 1)
    tallies = tallies.at[donor].add(-moved).at[taker].add(moved)
    items = jnp.searchsorted(jnp.cumsum(tallies), jnp.arange(rows * top), side="right").astype(jnp.int32)
    listing = items.reshape(top, rows).T
    listing = listing[jax.random.permutation(jax.random.fold_in(own, 1), rows)]
    rotation = jax.random.randint(jax.random.fold_in(own, 2), (rows, 1), 0, top)
    return jnp.take_along_axis(listing, (jnp.arange(top)[None, :] + rotation) % top, axis=1)


def portions_of(count, total, reach, skew, full):
    loads = [(1 << 20) // math.isqrt(rank ** skew) + 1 for rank in range(1, count + 1)]
    largest = reach if full else min(reach, max(-(-total // count), total * loads[0] // sum(loads)))
    least = 1 if total - largest >= count - 1 else 0
    holding, spare = [largest] + [least] * (count - 1), total - largest - least * (count - 1)
    while spare > 0:
        movable = [i for i in range(1, count) if holding[i] < largest] or [i for i in range(1, count) if holding[i] < reach]
        mass, budget = sum([loads[i] for i in movable]), spare
        for i in movable:
            more = min(reach - holding[i], max(1, budget * loads[i] // mass), spare)
            holding[i] = holding[i] + more
            spare = spare - more
    return np.array(holding)


def bell_draw(rng, shape, width, bound, pieces=(), kind=jnp.bfloat16):
    drawn = width * jax.random.normal(rng, shape, jnp.float32)
    if pieces:
        drawn = drawn * steps_of(rng, shape, pieces, -0.22, 0.18)
    return jnp.clip(drawn, -bound, bound).astype(kind)


def setup_inputs(seed: int = 0) -> dict:
    arg_keys = jax.random.split(jax.random.key(seed), 12)
    images_in = bell_draw(arg_keys[0], (MICRO, IMAGES, SEQ, D), 1.0, 6.0, ((1, 64),))
    cotangent = bell_draw(arg_keys[1], (MICRO, IMAGES, SEQ, D), 1.0, 6.0, ((1, 64),))
    gain_one = jnp.clip(1.0 + 0.18 * jax.random.normal(arg_keys[2], (SECTIONS, D), jnp.float32), 0.1, 1.9)
    w_qkv = bell_draw(arg_keys[3], (SECTIONS, D, 3 * D), D ** -0.5, 0.3125, ((0, 2),))
    w_out = bell_draw(arg_keys[4], (SECTIONS, D, D), (D // 32) ** -0.5, 1.75, ((0, 2),))
    gain_two = jnp.clip(1.0 + 0.18 * jax.random.normal(arg_keys[5], (SECTIONS, D), jnp.float32), 0.1, 1.9)
    w_router = bell_draw(arg_keys[6], (SECTIONS, D, EXPERTS), (2 * D) ** -0.5, 0.21875, ((0, 2),), jnp.float32)
    w_in = bell_draw(arg_keys[7], (SECTIONS, EXPERTS, D, FF), D ** -0.5, 0.3125, ((0, 2), (1, 32)))
    w_back = bell_draw(arg_keys[8], (SECTIONS, EXPERTS, FF, D), (FF // 256 + 1) ** -0.5, 2.0, ((0, 2), (1, 32)))
    routes_keys = jax.random.split(jax.random.fold_in(arg_keys[9], 1), SECTIONS * MICRO * IMAGES * SEQ // (IMG_DEV * SEQ))
    routes_turns = jax.random.permutation(jax.random.fold_in(arg_keys[9], 3), SECTIONS * MICRO * IMAGES * SEQ // (IMG_DEV * SEQ))
    routes = jax.vmap(lambda own, number: shared_out(jax.random.fold_in(arg_keys[9], 2), own, number, IMG_DEV * SEQ, EXPERTS, 2, CAP, 1))(routes_keys, routes_turns).reshape((SECTIONS, MICRO, IMAGES, SEQ, 2))
    keep = set_ends((jax.random.randint(arg_keys[10], (SECTIONS, MICRO, IMAGES, SEQ, 2), 0, 8) < 7).astype(jnp.int32), jax.random.fold_in(arg_keys[10], 1), 0, 1)
    return dict(images_in=images_in, cotangent=cotangent, gain_one=gain_one, w_qkv=w_qkv, w_out=w_out, gain_two=gain_two, w_router=w_router, w_in=w_in, w_back=w_back, routes=routes, keep=keep)


@jax.custom_vjp
def low(v):
    return lax.optimization_barrier(v.astype(jnp.bfloat16)).astype(jnp.float32)

@jax.custom_vjp
def low_back(v):
    return v

def low_keep(v):
    return (low(v), None)

def low_pass(kept, grad):
    return (grad,)

def back_keep(v):
    return (v, None)

def back_low(kept, grad):
    return (low(grad),)
low.defvjp(low_keep, low_pass)
low_back.defvjp(back_keep, back_low)
EPSILON = 1e-06
HIGHEST = lax.Precision.HIGHEST

def layer_norm(values, gain):
    center = values - lax.optimization_barrier(jnp.mean(values, axis=-1, keepdims=True))
    spread = lax.optimization_barrier(jnp.mean(center * center, axis=-1, keepdims=True))
    return center * lax.rsqrt(spread + EPSILON) * gain

def attend(qkv):
    query = qkv[:, :D].reshape(SEQ, HEADS, HEAD)
    keys = qkv[:, D:2 * D].reshape(SEQ, HEADS, HEAD)
    values = qkv[:, 2 * D:].reshape(SEQ, HEADS, HEAD)
    scores = low_back(jnp.einsum('shd,thd->hst', query, keys, precision=HIGHEST) * HEAD ** (-0.5))
    weights = low(jax.nn.softmax(scores, axis=-1))
    return jnp.einsum('hst,thd->shd', weights, values, precision=HIGHEST).reshape(SEQ, D)

def run_expert(items):
    rows, first_weight, second_weight = items
    hidden = low_back(jnp.dot(rows, first_weight, precision=HIGHEST))
    active = low(jax.nn.gelu(hidden, approximate=False))
    return low_back(low(jnp.dot(active, second_weight, precision=HIGHEST)))

def block(xin, routes, keep, gain_one, w_qkv, w_out, gain_two, w_router, w_in, w_back):
    normed = low(layer_norm(xin, gain_one))
    qkv = low_back(low(jnp.einsum('isd,de->ise', normed, w_qkv, precision=HIGHEST)))
    attended = low_back(low(lax.map(jax.checkpoint(attend), qkv)))
    mixed = xin + low_back(jnp.einsum('isd,de->ise', attended, w_out, precision=HIGHEST))
    second = layer_norm(mixed, gain_two)
    probs = jax.nn.softmax(jnp.einsum('isd,de->ise', second, w_router, precision=HIGHEST), axis=-1)
    groups = routes.reshape(N_EXPERT, N_DP, IMG_DEV * SEQ * 2).astype(jnp.int32)
    marks = (groups[..., None] == jnp.arange(EXPERTS, dtype=jnp.int32)).astype(jnp.int32)
    before = jnp.cumsum(marks, axis=2) - marks
    slot = lax.optimization_barrier(jnp.sum(before * marks, axis=3))
    source = jnp.arange(N_EXPERT, dtype=jnp.int32)[:, None, None]
    member = jnp.arange(N_DP, dtype=jnp.int32)[None, :, None]
    place = (((groups * N_DP + member) * N_EXPERT + source) * CAP + slot).reshape(-1).astype(jnp.int32)
    pairs = routes.reshape(-1, 2).astype(jnp.int32)
    chosen = (pairs[:, :, None] == jnp.arange(EXPERTS, dtype=jnp.int32)).astype(jnp.float32)
    gates = lax.optimization_barrier(jnp.sum(chosen * probs.reshape(-1, 1, EXPERTS), axis=2)) * keep.reshape(-1, 2).astype(jnp.float32)
    rows = jnp.repeat(low(second).reshape(-1, D), 2, axis=0)
    buffer = jnp.zeros((EXPERTS * N_DP * N_EXPERT * CAP, D), jnp.float32).at[place].add(rows)
    buffer = low_back(buffer)
    produced = lax.map(jax.checkpoint(run_expert), (buffer.reshape(EXPERTS, N_DP * N_EXPERT * CAP, D), w_in, w_back))
    picked = produced.reshape(-1, D)[place].reshape(-1, 2, D)
    combined = lax.optimization_barrier(jnp.sum(gates[:, :, None] * picked, axis=1))
    return mixed + combined.reshape(mixed.shape)

def forward(images_in, probe, gain_one, w_qkv, w_out, gain_two, w_router, w_in, w_back, routes, keep):
    firsts = []
    seconds = []
    for micro in range(MICRO):
        sectioned = block(images_in[micro], routes[0, micro], keep[0, micro], gain_one[0], w_qkv[0], w_out[0], gain_two[0], w_router[0], w_in[0], w_back[0])
        sectioned = low_back(low(sectioned) + probe[micro])
        final = low(block(sectioned, routes[1, micro], keep[1, micro], gain_one[1], w_qkv[1], w_out[1], gain_two[1], w_router[1], w_in[1], w_back[1]))
        firsts.append(sectioned)
        seconds.append(final)
    return (jnp.stack(firsts), jnp.stack(seconds))

def reference(images_in, cotangent, gain_one, w_qkv, w_out, gain_two, w_router, w_in, w_back, routes, keep):
    floats = (images_in.astype(jnp.float32), jnp.zeros(images_in.shape, jnp.float32), gain_one, w_qkv.astype(jnp.float32), w_out.astype(jnp.float32), gain_two, w_router, w_in.astype(jnp.float32), w_back.astype(jnp.float32))

    def run(*values):
        return forward(*values, routes, keep)
    outputs, pull = jax.vjp(run, *floats)
    firsts, seconds = outputs
    grads = pull((jnp.zeros_like(firsts), cotangent.astype(jnp.float32)))
    activations = jnp.stack([firsts, seconds]).astype(jnp.bfloat16)
    input_grad = jnp.stack([grads[0], grads[1]])
    return (activations, input_grad, grads[2], grads[3], grads[4], grads[5], grads[6], grads[7], grads[8])
```

```python
import math

import jax
import jax.numpy as jnp
from jax import lax
from jax.experimental import pallas as pl
from jax.experimental.pallas import tpu as pltpu
from jax.sharding import PartitionSpec as P

HEADS = 6
HEAD = 64
PAIR = 2 * HEAD
SCALE = HEAD ** (-0.5)
EPSILON = 1e-06
HIGHEST = lax.Precision.HIGHEST
BF = jnp.bfloat16
F32 = jnp.float32
LANE = 128
MAIN = 16
TAIL = 4
KP = 256
CHUNK = 256
MESH = pl.DeviceIdType.MESH


def mm(a, b, precision=None):
    return lax.dot_general(a, b, (((1,), (0,)), ((), ())), precision=precision, preferred_element_type=F32)


def mm_nt(a, b, precision=None):
    return lax.dot_general(a, b, (((1,), (1,)), ((), ())), precision=precision, preferred_element_type=F32)


def mm_tn(a, b, precision=None):
    return lax.dot_general(a, b, (((0,), (0,)), ((), ())), precision=precision, preferred_element_type=F32)


def iota(shape, dim):
    return lax.broadcasted_iota(jnp.int32, shape, dim)


def one_hot(hit, dtype=BF):
    return jnp.where(hit, 1.0, 0.0).astype(dtype)


def gelu_parts(h):
    z = jnp.abs(h) * (0.5**0.5)
    t = 1.0 / (1.0 + 0.3275911 * z)
    ex = jnp.exp(-(z * z))
    poly = t * (0.127414796 + t * (-0.142248368 + t * (0.7107068705 + t * (-0.7265760135 + t * 0.5307027145))))
    q = poly * ex
    phi = jnp.where(h >= 0.0, 1.0 - q, q)
    return h * phi, phi + h * (ex * (1.0 / math.sqrt(2.0 * math.pi)))


def norm_parts(x):
    cen = x - jnp.mean(x, axis=-1, keepdims=True)
    rstd = lax.rsqrt(jnp.mean(cen * cen, axis=-1, keepdims=True) + EPSILON)
    return cen * rstd, rstd


def norm_back(d_hat, hat, rstd):
    return rstd * (
        d_hat
        - jnp.mean(d_hat, axis=-1, keepdims=True)
        - hat * jnp.mean(d_hat * hat, axis=-1, keepdims=True)
    )


def kernel(dims, *refs):
    seq, width, ff, ne = dims
    t_rows = -(-seq // 16) * 16
    rm, rt = ne * MAIN, ne * TAIL
    rows = rm + rt
    bits = ne.bit_length() - 1
    (
        images, cot, meta, small, w_qkv, w_out, w_in, w_back,
        act_o, ig_o, dense_o, sm_o, wi_o, wi2_o, wb_o, wb2_o,
        meta_s, small_s, wqkv_s, wout_s, win_s, wback_s,
        st_s, s_s, xh1, rs1, xh2, rs2, nrm, qs, ps, att, mix, sec, sec_f, prb, cols_s, gate_s, pk, dd, dt,
        tx, rx, in_s, ac_s, dg_s, dh_s, dp_s, ret, acc, vs, dsr, dbr, dqkv, dmx, ya, ya_rx, gx, gx_rx,
        wtx_i, wtx_b, wrc_i, wrc_b, wrd_i, wrd_b,
        den, den_rc, smt, sm_rc, rs_rx, smrs_rx, dpt, dpr, smdpt, smdpr, agt, ag_rx, smag, smag_rx, dfin, smfin,
        wsem, wsend, a2s, a2r, cxs, cxr, dps, dpr_sem, rss, rsr, ags, agr, acs, acr, igs, igr, osem,
    ) = refs
    core = lax.axis_index("section")
    me = lax.axis_index("expert")
    half = lax.axis_index("dp")
    other = 1 - core

    def expert_at(k):
        return lax.rem(me + k, ne)

    def wait(ref, sem):
        pltpu.make_async_copy(ref, ref, sem).wait()

    def to_core(src, dst, send, recv):
        return pltpu.make_async_remote_copy(
            src_ref=src, dst_ref=dst, send_sem=send, recv_sem=recv,
            device_id={"section": other}, device_id_type=MESH,
        )

    def to_dp(src, dst, send, recv):
        return pltpu.make_async_remote_copy(
            src_ref=src, dst_ref=dst, send_sem=send, recv_sem=recv,
            device_id={"dp": 1 - half}, device_id_type=MESH,
        )

    barrier = pltpu.get_barrier_semaphore()

    def greet(k, _):
        pl.semaphore_signal(barrier, inc=1, device_id={"expert": expert_at(k)}, device_id_type=MESH)
        return _

    lax.fori_loop(1, ne, greet, 0)
    pl.semaphore_signal(barrier, inc=1, device_id={"section": other}, device_id_type=MESH)
    pl.semaphore_signal(barrier, inc=1, device_id={"dp": 1 - half}, device_id_type=MESH)

    held = [
        (meta.at[core], meta.at[other], meta_s),
        (small, small, small_s),
        (w_qkv.at[0], w_qkv.at[0], wqkv_s),
        (w_out.at[0], w_out.at[0], wout_s),
        (w_in.at[0, 0], w_in.at[0, 0], win_s),
        (w_back.at[0, 0], w_back.at[0, 0], wback_s),
    ]
    for i, (mine, _, dst) in enumerate(held):
        pltpu.make_async_copy(mine, dst.at[core], wsem.at[core, i]).start()

    for ref in (nrm, qs, att, sec):
        for b in range(2):
            ref[b, t_rows:KP, :] = jnp.zeros((KP - t_rows, ref.shape[2]), BF)
    for ref in (dbr, dqkv):
        ref[t_rows:KP, :] = jnp.zeros((KP - t_rows, ref.shape[1]), BF)
    for b in range(2):
        vs[b, t_rows:KP, :] = jnp.zeros((KP - t_rows, width), BF)
    smt[...] = jnp.zeros(smt.shape, F32)
    row, col = iota((rm, 3 * rt), 0), iota((rm, 3 * rt), 1)
    chunk = (col >= rt).astype(jnp.int32) + (col >= 2 * rt).astype(jnp.int32)
    n = col - chunk * rt
    st_s[...] = one_hot(((row >> 4) == (n & (ne - 1))) & ((row & 15) == 4 * chunk + (n >> bits)))
    row, col = iota((3 * rt, rm), 0), iota((3 * rt, rm), 1)
    chunk = (row >= rt).astype(jnp.int32) + (row >= 2 * rt).astype(jnp.int32)
    n = row - chunk * rt
    s_s[...] = one_hot(((col >> 4) == (n & (ne - 1))) & ((col & 15) == 4 * chunk + (n >> bits)))

    def padded(value):
        gx[0, t_rows - 16:t_rows, :] = jnp.zeros((16, width), F32)
        gx[0, 0:seq, :] = value.astype(F32)
        return gx[0, 0:t_rows, :]

    pl.semaphore_wait(barrier, ne + 1)
    for i, (_, theirs, dst) in enumerate(held):
        to_core(theirs, dst.at[core], wsend.at[i], wsem.at[core, i]).start()

    def weight(b, i):
        wait(held[i][2].at[b], wsem.at[b, i])

    def pack(phase, main, tail):
        for c in range(3):
            tx[phase, :, 16 * c:16 * c + 16, :] = main[:, LANE * c:LANE * c + LANE].reshape(ne, 16, LANE)
        stack = jnp.concatenate([tail[:, LANE * c:LANE * c + LANE] for c in range(3)], axis=0)
        tx[phase, :, 48:64, :] = mm(st_s[...], stack).astype(BF).reshape(ne, 16, LANE)

    def unpack(phase, out):
        for c in range(3):
            out[0:rm, LANE * c:LANE * c + LANE] = rx[phase, :, 16 * c:16 * c + 16, :].reshape(rm, LANE)
        tail = mm(s_s[...], rx[phase, :, 48:64, :].reshape(rm, LANE)).astype(BF)
        for c in range(3):
            out[rm:rows, LANE * c:LANE * c + LANE] = tail[c * rt:c * rt + rt]

    def exchange(phase):
        def step(k, _):
            pltpu.make_async_remote_copy(
                src_ref=tx.at[phase, k], dst_ref=rx.at[phase, ne - k],
                send_sem=a2s.at[phase], recv_sem=a2r.at[phase],
                device_id={"expert": expert_at(k)}, device_id_type=MESH,
            ).start()
            return _

        lax.fori_loop(1, ne, step, 0)
        rx[phase, 0] = tx[phase, 0]

    def arrived(phase):
        wait(rx.at[phase, pl.ds(1, ne - 1)], a2r.at[phase])

    def place_of(rank, slot):
        return jnp.where(slot < MAIN, rank * MAIN + slot, rm + (slot - MAIN) * ne + rank)

    def route(b):
        data = meta_s[b]
        mef = me.astype(F32)
        chosen, keeps = [data[0:1], data[1:2]], [data[2:3], data[3:4]]
        rank = [r - mef for r in chosen]
        rank = [jnp.where(r < 0.0, r + ne, r) for r in rank]
        lanes = iota((ne, KP), 0).astype(F32)
        marks = [one_hot(lanes == r, F32) for r in rank]
        earlier = one_hot(iota((KP, KP), 0) < iota((KP, KP), 1))
        before = mm((marks[0] + marks[1]).astype(BF), earlier)
        slot = [jnp.sum(before * m, axis=0, keepdims=True) for m in marks]
        spot = iota((rows, KP), 0).astype(F32)
        for k in range(2):
            dt[b, :, KP * k:KP * k + KP] = one_hot(spot == place_of(rank[k], slot[k]))
        which = iota((8, KP), 0)
        lines = jnp.zeros((8, KP), F32)
        for i, line in enumerate((*rank, *slot, *keeps, *chosen)):
            lines = jnp.where(which == i, line, lines)
        same = one_hot(iota((t_rows, KP), 0) == iota((t_rows, KP), 1))
        cols = mm_nt(same, lines.astype(BF))
        cols_s[b] = cols
        spot = iota((t_rows, rows), 1).astype(F32)
        for k in range(2):
            dd[b, k] = one_hot(spot == place_of(cols[:, k:k + 1], cols[:, 2 + k:3 + k]))

    def chosen_marks(b):
        lanes = iota((t_rows, ne), 1).astype(F32)
        return [one_hot(lanes == cols_s[b, :, 6 + k:7 + k], F32) * cols_s[b, :, 4 + k:5 + k] for k in range(2)]

    def head_masks():
        lanes = iota((1, PAIR), 1)
        return [one_hot(lanes < HEAD), one_hot(lanes >= HEAD)]

    def forward_dense(b, x):
        hat, rstd = norm_parts(x)
        xh1[b], rs1[b] = hat, rstd
        normed = (hat * small_s[b, ne:ne + 1, :]).astype(BF)
        nrm[b, 0:t_rows, :] = normed
        weight(b, 2)
        qs[b, 0:t_rows, :] = mm(normed, wqkv_s[b]).astype(BF)
        masks = head_masks()
        real = iota((t_rows, KP), 1) < seq
        for p in range(HEADS // 2):
            at = PAIR * p
            query, key = qs[b, 0:t_rows, at:at + PAIR], qs[b, :, width + at:width + at + PAIR]
            value = qs[b, :, 2 * width + at:2 * width + at + PAIR]
            out = jnp.zeros((t_rows, PAIR), F32)
            for h in range(2):
                scores = mm_nt(query * masks[h], key) * SCALE
                scores = jnp.where(real, scores, -1e30)
                e = jnp.exp(scores - jnp.max(scores, axis=-1, keepdims=True))
                probs = e * (1.0 / jnp.sum(e, axis=-1, keepdims=True))
                ps[b, 2 * p + h] = probs
                out = out + mm(probs.astype(BF), value * masks[h])
            att[b, 0:t_rows, at:at + PAIR] = out.astype(BF)
        weight(b, 3)
        mixed = x + mm(att[b, 0:t_rows, :], wout_s[b])
        mix[b] = mixed
        hat, rstd = norm_parts(mixed)
        xh2[b], rs2[b] = hat, rstd
        second = hat * small_s[b, ne + 1:ne + 2, :]
        sec_f[b] = second
        sec[b, 0:t_rows, :] = second.astype(BF)
        spread = dt[b, :, 0:KP] + dt[b, :, KP:2 * KP]
        pack(4 * b, mm(spread[0:rm], sec[b]).astype(BF), mm(spread[rm:rows], sec[b]).astype(BF))
        exchange(4 * b)
        logits = mm_nt(second, small_s[b, 0:ne, :], HIGHEST)
        e = jnp.exp(logits - jnp.max(logits, axis=-1, keepdims=True))
        probs = e / jnp.sum(e, axis=-1, keepdims=True)
        prb[b] = probs
        for k, marks in enumerate(chosen_marks(b)):
            gate_s[b, k] = jnp.sum(marks * probs, axis=-1, keepdims=True)

    def forward_expert(b):
        weight(b, 4)
        weight(b, 5)
        arrived(4 * b)
        unpack(4 * b, in_s.at[b])
        acc[...] = jnp.zeros(acc.shape, F32)

        def step(i, _):
            at = pl.ds(pl.multiple_of(i * CHUNK, CHUNK), CHUNK)
            active, slope = gelu_parts(mm(in_s[b], win_s[b, :, at]))
            active = active.astype(BF)
            ac_s[b, :, at] = active
            dg_s[b, :, at] = slope.astype(BF)
            acc[...] += mm(active, wback_s[b, at, :])
            return _

        lax.fori_loop(0, ff // CHUNK, step, 0)
        pack(4 * b + 1, acc[0:rm, :].astype(BF), acc[rm:rows, :].astype(BF))
        exchange(4 * b + 1)

    def forward_combine(b):
        arrived(4 * b + 1)
        unpack(4 * b + 1, ret)
        y = mix[b]
        for k in range(2):
            picked = mm(dd[b, k], ret[...])
            pk[b, k] = picked.astype(BF)
            y = y + gate_s[b, k] * picked
        low = y.astype(BF)
        ya[b] = low
        return low.astype(F32)

    def backward_start(b, dy):
        d_probs = jnp.zeros((t_rows, ne), F32)
        for k, marks in enumerate(chosen_marks(b)):
            d_gate = jnp.sum(dy * pk[b, k].astype(F32), axis=-1, keepdims=True)
            d_probs = d_probs + marks * d_gate
            vs[k, 0:t_rows, :] = (gate_s[b, k] * dy).astype(BF)
        stacked = vs[...].reshape(2 * KP, width)
        pack(4 * b + 2, mm(dt[b, 0:rm], stacked).astype(BF), mm(dt[b, rm:rows], stacked).astype(BF))
        exchange(4 * b + 2)
        probs = prb[b]
        d_logits = probs * (d_probs - jnp.sum(probs * d_probs, axis=-1, keepdims=True))
        dsr[...] = mm(d_logits, small_s[b, 0:ne, :], HIGHEST)
        return mm_tn(d_logits, sec_f[b], HIGHEST)

    def backward_expert(b):
        arrived(4 * b + 2)
        unpack(4 * b + 2, dp_s)
        acc[...] = jnp.zeros(acc.shape, F32)

        def step(i, _):
            at = pl.ds(pl.multiple_of(i * CHUNK, CHUNK), CHUNK)
            d_hidden = (mm_nt(dp_s[...], wback_s[b, at, :]) * dg_s[b, :, at].astype(F32)).astype(BF)
            dh_s[:, at] = d_hidden
            acc[...] += mm_nt(d_hidden, win_s[b, :, at])
            return _

        lax.fori_loop(0, ff // CHUNK, step, 0)
        pack(4 * b + 3, acc[0:rm, :].astype(BF), acc[rm:rows, :].astype(BF))
        exchange(4 * b + 3)

    def expert_grads(b):
        def step(i, _):
            at = pl.ds(pl.multiple_of(i * CHUNK, CHUNK), CHUNK)
            wtx_i[:, at] = mm_tn(in_s[b], dh_s[:, at]).astype(BF)
            wtx_b[at, :] = mm_tn(ac_s[b, :, at], dp_s[...]).astype(BF)
            return _

        lax.fori_loop(0, ff // CHUNK, step, 0)

        @pl.when(core != b)
        def _():
            to_core(wtx_i, wrc_i, cxs.at[0], cxr.at[0]).start()
            to_core(wtx_b, wrc_b, cxs.at[1], cxr.at[1]).start()

        @pl.when(core == b)
        def _():
            wait(wrc_i, cxr.at[0])
            wtx_i[...] = (wtx_i[...].astype(F32) + wrc_i[...].astype(F32)).astype(BF)
            to_dp(wtx_i, wrd_i, dps.at[0], dpr_sem.at[0]).start()
            pltpu.make_async_copy(wtx_i, wi_o, osem.at[0]).start()
            wait(wrc_b, cxr.at[1])
            wtx_b[...] = (wtx_b[...].astype(F32) + wrc_b[...].astype(F32)).astype(BF)
            to_dp(wtx_b, wrd_b, dps.at[1], dpr_sem.at[1]).start()
            pltpu.make_async_copy(wtx_b, wb_o, osem.at[1]).start()

    def grads_sent(b):
        @pl.when(core != b)
        def _():
            wait(wtx_i, cxs.at[0])
            wait(wtx_b, cxs.at[1])
            wait(den, cxs.at[2])
            wait(smt, cxs.at[3])

        @pl.when(core == b)
        def _():
            wait(wtx_i, dps.at[0])
            wait(wtx_b, dps.at[1])
            wait(wi_o, osem.at[0])
            wait(wb_o, osem.at[1])

    def backward_dense(b, dy, d_router):
        arrived(4 * b + 3)
        unpack(4 * b + 3, ret)
        d_second = mm(dd[b, 0] + dd[b, 1], ret[...]) + dsr[...]
        hat2 = xh2[b]
        d_gain_two = jnp.sum(d_second * hat2, axis=0, keepdims=True)
        d_mixed = dy + norm_back(d_second * small_s[b, ne + 1:ne + 2, :], hat2, rs2[b])
        dmx[...] = d_mixed
        d_branch = d_mixed.astype(BF)
        dbr[0:t_rows, :] = d_branch
        piece = width * 4 // ne
        per = ne // 4
        den[3 * per:4 * per] = mm_tn(att[b], dbr[...]).astype(BF).reshape(per, piece, width)
        d_att = mm_nt(d_branch, wout_s[b]).astype(BF)
        masks = head_masks()
        for p in range(HEADS // 2):
            at = PAIR * p
            query, key = qs[b, 0:t_rows, at:at + PAIR], qs[b, :, width + at:width + at + PAIR]
            value = qs[b, :, 2 * width + at:2 * width + at + PAIR]
            d_query = jnp.zeros((t_rows, PAIR), F32)
            d_key = jnp.zeros((KP, PAIR), F32)
            d_value = jnp.zeros((KP, PAIR), F32)
            for h in range(2):
                d_out = d_att[:, at:at + PAIR] * masks[h]
                probs = ps[b, 2 * p + h]
                d_value = d_value + mm_tn(probs.astype(BF), d_out)
                d_probs = mm_nt(d_out, value)
                inner = jnp.sum(probs * d_probs, axis=-1, keepdims=True)
                d_scores = (probs * (d_probs - inner)).astype(BF)
                d_query = d_query + mm(d_scores, key * masks[h])
                d_key = d_key + mm_tn(d_scores, query * masks[h])
            dqkv[0:t_rows, at:at + PAIR] = (d_query * SCALE).astype(BF)
            dqkv[:, width + at:width + at + PAIR] = (d_key * SCALE).astype(BF)
            dqkv[:, 2 * width + at:2 * width + at + PAIR] = d_value.astype(BF)
        d_normed = mm_nt(dqkv[0:t_rows, :], wqkv_s[b])
        hat1 = xh1[b]
        d_gain_one = jnp.sum(d_normed * hat1, axis=0, keepdims=True)
        d_x = dmx[...] + norm_back(d_normed * small_s[b, ne:ne + 1, :], hat1, rs1[b])
        for q in range(3):
            grad = mm_tn(nrm[b], dqkv[:, width * q:width * q + width])
            den[q * per:q * per + per] = grad.astype(BF).reshape(per, piece, width)
        for c in range(3):
            at = LANE * c
            smt[:, c, :] = d_router[:, at:at + LANE]
            smt[c, 3:4, :] = d_gain_one[:, at:at + LANE]
            smt[c, 4:5, :] = d_gain_two[:, at:at + LANE]

        @pl.when(core != b)
        def _():
            to_core(den, den_rc, cxs.at[2], cxr.at[2]).start()
            to_core(smt, sm_rc, cxs.at[3], cxr.at[3]).start()

        return d_x

    def dense_scatter(b):
        @pl.when(core == b)
        def _():
            wait(den_rc, cxr.at[2])
            den[...] = (den[...].astype(F32) + den_rc[...].astype(F32)).astype(BF)
            wait(sm_rc, cxr.at[3])
            smt[...] = smt[...] + sm_rc[...]

            def step(k, _):
                to = expert_at(k)
                pltpu.make_async_remote_copy(
                    src_ref=den.at[to], dst_ref=rs_rx.at[ne - k], send_sem=rss.at[0], recv_sem=rsr.at[0],
                    device_id={"expert": to}, device_id_type=MESH,
                ).start()
                pltpu.make_async_remote_copy(
                    src_ref=smt.at[to], dst_ref=smrs_rx.at[ne - k], send_sem=rss.at[1], recv_sem=rsr.at[1],
                    device_id={"expert": to}, device_id_type=MESH,
                ).start()
                return _

            lax.fori_loop(1, ne, step, 0)

    def dense_reduce(b):
        @pl.when(core == b)
        def _():
            peers = pl.ds(1, ne - 1)
            wait(rs_rx.at[peers], rsr.at[0])
            wait(smrs_rx.at[peers], rsr.at[1])
            dpt[...] = den[me].astype(F32)
            smdpt[...] = smt[me]

            def step(k, _):
                dpt[...] += rs_rx[k].astype(F32)
                smdpt[...] += smrs_rx[k]
                return _

            lax.fori_loop(1, ne, step, 0)
            to_dp(dpt, dpr, dps.at[2], dpr_sem.at[2]).start()
            to_dp(smdpt, smdpr, dps.at[3], dpr_sem.at[3]).start()
            wait(rs_rx.at[peers], rss.at[0])
            wait(smrs_rx.at[peers], rss.at[1])

    def dense_gather(b):
        @pl.when(core == b)
        def _():
            wait(dpr, dpr_sem.at[2])
            wait(smdpr, dpr_sem.at[3])
            agt[...] = (dpt[...] + dpr[...]).astype(BF)
            smag[...] = smdpt[...] + smdpr[...]

            def step(k, _):
                to = expert_at(k)
                pltpu.make_async_remote_copy(
                    src_ref=agt, dst_ref=ag_rx.at[ne - k], send_sem=ags.at[0], recv_sem=agr.at[0],
                    device_id={"expert": to}, device_id_type=MESH,
                ).start()
                pltpu.make_async_remote_copy(
                    src_ref=smag, dst_ref=smag_rx.at[ne - k], send_sem=ags.at[1], recv_sem=agr.at[1],
                    device_id={"expert": to}, device_id_type=MESH,
                ).start()
                return _

            lax.fori_loop(1, ne, step, 0)
            dfin[me] = agt[...]
            smfin[me] = smag[...]

    def dense_finish(b):
        @pl.when(core == b)
        def _():
            peers = pl.ds(1, ne - 1)
            wait(ag_rx.at[peers], agr.at[0])
            wait(smag_rx.at[peers], agr.at[1])

            def step(k, _):
                dfin[expert_at(k)] = ag_rx[k]
                smfin[expert_at(k)] = smag_rx[k]
                return _

            lax.fori_loop(1, ne, step, 0)
            pltpu.make_async_copy(dfin, dense_o, osem.at[2]).start()
            pltpu.make_async_copy(smfin, sm_o, osem.at[3]).start()
            wait(ag_rx.at[peers], ags.at[0])
            wait(smag_rx.at[peers], ags.at[1])
            wait(dpt, dps.at[2])
            wait(smdpt, dps.at[3])

    for b in range(2):
        weight(b, 0)
        weight(b, 1)
        route(b)
        if b == 0:
            x = padded(images[core, 0])
        forward_dense(b, x)
        forward_expert(b)
        x = forward_combine(b)
    to_core(ya.at[other], ya_rx, acs, acr).start()
    dy = padded(cot[core, 0])
    dmx[...] = dy
    dy = dmx[...]
    for b in (1, 0):
        d_router = backward_start(b, dy)
        if b == 0:
            dense_reduce(1)
        backward_expert(b)
        if b == 0:
            dense_gather(1)
            grads_sent(1)
        expert_grads(b)
        dx = backward_dense(b, dy, d_router)
        if b == 1:
            dy = dx.astype(BF).astype(F32)
            gx[1] = dy
            dense_scatter(1)
        else:
            gx[0] = dx
    to_core(gx.at[other], gx_rx, igs, igr).start()
    dense_scatter(0)
    dense_finish(1)
    dense_reduce(0)
    dense_gather(0)
    wait(ya_rx, acr)
    pltpu.make_async_copy(ya.at[core], act_o.at[core], osem.at[4]).start()
    pltpu.make_async_copy(ya_rx, act_o.at[other], osem.at[5]).start()
    wait(gx_rx, igr)
    pltpu.make_async_copy(gx.at[core], ig_o.at[core], osem.at[6]).start()
    pltpu.make_async_copy(gx_rx, ig_o.at[other], osem.at[7]).start()
    wait(wrd_i, dpr_sem.at[0])
    pltpu.make_async_copy(wrd_i, wi2_o, osem.at[8]).start()
    wait(wrd_b, dpr_sem.at[1])
    pltpu.make_async_copy(wrd_b, wb2_o, osem.at[9]).start()
    dense_finish(0)
    grads_sent(0)
    for i, (_, theirs, _dst) in enumerate(held):
        wait(theirs, wsend.at[i])
    for phase in range(8):
        wait(tx.at[phase, pl.ds(1, ne - 1)], a2s.at[phase])
    wait(ya.at[other], acs)
    wait(gx.at[other], igs)
    for i, ref in enumerate((dense_o, sm_o, act_o.at[0], act_o.at[0], ig_o.at[0], ig_o.at[0], wi2_o, wb2_o)):
        wait(ref, osem.at[2 + i])


def body(images_in, cotangent, gain_one, w_qkv, w_out, gain_two, w_router, w_in, w_back, routes, keep):
    micro, _, seq, width = images_in.shape
    ne = lax.axis_size("expert")
    ff = w_in.shape[3]
    t_rows = -(-seq // 16) * 16
    rm, rt = ne * MAIN, ne * TAIL
    rows = rm + rt
    piece = 4 * width // ne
    pad = ((0, 0), (0, 0), (0, KP - seq))
    chosen = jnp.pad(jnp.swapaxes(routes[0, :, 0], 1, 2).astype(F32), pad, constant_values=-64.0)
    kept = jnp.pad(jnp.swapaxes(keep[0, :, 0], 1, 2).astype(F32), pad)
    meta = jnp.concatenate([chosen, kept, jnp.zeros((micro, 4, KP), F32)], axis=1)
    small = jnp.concatenate([w_router[0].T, gain_one, gain_two, jnp.zeros((6, width), F32)], axis=0)
    vmem, anywhere = pl.BlockSpec(memory_space=pltpu.VMEM), pl.BlockSpec(memory_space=pl.ANY)
    dma = pltpu.SemaphoreType.DMA

    def v(*shape, dtype=BF):
        return pltpu.VMEM(shape, dtype)

    t, r, w = t_rows, rows, width
    scratch = [
        v(2, 8, KP, dtype=F32), v(2, ne + 8, w, dtype=F32),
        v(2, w, 3 * w), v(2, w, w), v(2, w, ff), v(2, ff, w),
        v(rm, 3 * rt), v(3 * rt, rm),
        v(2, t, w, dtype=F32), v(2, t, 1, dtype=F32), v(2, t, w, dtype=F32), v(2, t, 1, dtype=F32),
        v(2, KP, w), v(2, KP, 3 * w), v(2, HEADS, t, KP, dtype=F32), v(2, KP, w),
        v(2, t, w, dtype=F32), v(2, KP, w), v(2, t, w, dtype=F32), v(2, t, ne, dtype=F32),
        v(2, t, 8, dtype=F32), v(2, 2, t, 1, dtype=F32), v(2, 2, t, w), v(2, 2, t, r), v(2, r, 2 * KP),
        v(8, ne, 64, LANE), v(8, ne, 64, LANE), v(2, r, w), v(2, r, ff), v(2, r, ff), v(r, ff), v(r, w), v(r, w),
        v(r, w, dtype=F32), v(2, KP, w), v(t, w, dtype=F32), v(KP, w), v(KP, 3 * w), v(t, w, dtype=F32),
        v(2, t, w), v(t, w), v(2, t, w, dtype=F32), v(t, w, dtype=F32),
        v(w, ff), v(ff, w), v(w, ff), v(ff, w), v(w, ff), v(ff, w),
        v(ne, piece, w), v(ne, piece, w), v(ne, 8, LANE, dtype=F32), v(ne, 8, LANE, dtype=F32),
        v(ne, piece, w), v(ne, 8, LANE, dtype=F32),
        v(piece, w, dtype=F32), v(piece, w, dtype=F32), v(8, LANE, dtype=F32), v(8, LANE, dtype=F32),
        v(piece, w), v(ne, piece, w), v(8, LANE, dtype=F32), v(ne, 8, LANE, dtype=F32),
        v(ne, piece, w), v(ne, 8, LANE, dtype=F32),
        dma((2, 6)), dma((6,)), dma((8,)), dma((8,)), dma((4,)), dma((4,)), dma((4,)), dma((4,)),
        dma((2,)), dma((2,)), dma((2,)), dma((2,)), dma, dma, dma, dma, dma((10,)),
    ]
    shapes = [
        ((2, t, w), BF), ((2, t, w), F32), ((ne, piece, w), BF), ((ne, 8, LANE), F32),
        ((w, ff), BF), ((w, ff), BF), ((ff, w), BF), ((ff, w), BF),
    ]
    act, grad, dense, sm, wi, wi2, wb, wb2 = pl.pallas_call(
        lambda *refs: kernel((seq, width, ff, ne), *refs),
        out_shape=[jax.ShapeDtypeStruct(s, d) for s, d in shapes],
        in_specs=[vmem] * 4 + [anywhere] * 4,
        out_specs=[anywhere] * 8,
        scratch_shapes=scratch,
        compiler_params=pltpu.CompilerParams(
            collective_id=0, has_side_effects=True, vmem_limit_bytes=62 * 2**20
        ),
        name="blocks",
    )(images_in, cotangent, meta, small, w_qkv, w_out, w_in, w_back)
    dense = dense.reshape(4, width, width).astype(F32)
    d_w_qkv = jnp.concatenate([dense[0], dense[1], dense[2]], axis=1)
    d_router = sm[:, 0:3].reshape(ne, width).T
    return (
        act[None, :, None, :seq],
        grad[None, :, None, :seq],
        sm[0:3, 3].reshape(1, width),
        d_w_qkv[None],
        dense[3][None],
        sm[0:3, 4].reshape(1, width),
        d_router[None],
        (wi.astype(F32) + wi2.astype(F32))[None, None],
        (wb.astype(F32) + wb2.astype(F32))[None, None],
    )


def solution(mesh):
    spread = ("expert", "dp")
    tokens = P(None, spread, None, None)
    per_block = P("section", None, spread, None, None)
    vector, matrix, experts = P("section", None), P("section", None, None), P("section", "expert", None, None)
    return jax.shard_map(
        body,
        mesh=mesh,
        in_specs=(
            tokens, tokens, vector, matrix, matrix, vector, matrix, experts, experts, per_block, per_block,
        ),
        out_specs=(
            per_block, per_block, vector, matrix, matrix, vector, matrix, experts, experts,
        ),
        check_vma=False,
    )
```

```python
import math

import jax
import jax.numpy as jnp
from jax import lax
from jax.experimental import pallas as pl
from jax.experimental.pallas import tpu as pltpu
from jax.sharding import PartitionSpec as P

HEADS = 6
HEAD = 64
PAIR = 2 * HEAD
SCALE = HEAD ** (-0.5)
EPSILON = 1e-06
HIGHEST = lax.Precision.HIGHEST
BF = jnp.bfloat16
F32 = jnp.float32
LANE = 128
MAIN = 16
TAIL = 4
KP = 256
CHUNK = 512
ORDER = (0, 1, 4, 5, 6, 7, 2, 3)
GROUPS = 4
MESH = pl.DeviceIdType.MESH


def mm(a, b, precision=None):
    return lax.dot_general(a, b, (((1,), (0,)), ((), ())), precision=precision, preferred_element_type=F32)


def mm_nt(a, b, precision=None):
    return lax.dot_general(a, b, (((1,), (1,)), ((), ())), precision=precision, preferred_element_type=F32)


def mm_tn(a, b, precision=None):
    return lax.dot_general(a, b, (((0,), (0,)), ((), ())), precision=precision, preferred_element_type=F32)


def iota(shape, dim):
    return lax.broadcasted_iota(jnp.int32, shape, dim)


def one_hot(hit, dtype=BF):
    return jnp.where(hit, 1.0, 0.0).astype(dtype)


def phi_of(h):
    return 0.5 * lax.erf(h * (0.5**0.5)) + 0.5


def slope_of(h, phi):
    return phi + h * (jnp.exp(h * h * -0.5) * (1.0 / math.sqrt(2.0 * math.pi)))


def norm_parts(x):
    cen = x - jnp.mean(x, axis=-1, keepdims=True)
    rstd = lax.rsqrt(jnp.mean(cen * cen, axis=-1, keepdims=True) + EPSILON)
    return cen * rstd, rstd


def norm_back(d_hat, hat, rstd):
    return rstd * (
        d_hat
        - jnp.mean(d_hat, axis=-1, keepdims=True)
        - hat * jnp.mean(d_hat * hat, axis=-1, keepdims=True)
    )


def kernel(dims, *refs):
    seq, width, ff, ne = dims
    t_rows = -(-seq // 16) * 16
    gs = ne // GROUPS
    gm, gt = gs * MAIN, gs * TAIL
    gr = gm + gt
    rows = ne * (MAIN + TAIL)
    piece = width * 4 // ne
    per = ne // 4
    (
        images, cot, routes, keep, gain_one, gain_two, router, w_qkv, w_out, w_in, w_back,
        act_o, ig_o, qkv_o, out_o, sm_o, wi_o, wb_o,
        meta_m, meta_s, small_m, small_s, wqkv_s, wout_s, win_s, wback_s,
        s_s, xh1, rs1, xh2, rs2, nrm, qs, ps, att, mix, sec, prb, cols_s, gate_s, pk, dd, dt,
        tx, rx, in_s, ac_s, dg_s, dp_s, ret, vs, dsr, dbr, dqkv, dmx, ya, ya_rx, gx, gx_rx,
        wtx_i, wtx_b, wrc_i, wrc_b,
        den, den_rc, smt, rs_rx, dpt, dpr, agt, ag_rx, dfin_q, smfin,
        wsem, wsend, a2s, a2r, cxs, cxr, dps, dpr_sem, rss, rsr, ags, agr, acs, acr, igs, igr, osem,
    ) = refs
    core = lax.axis_index("section")
    me = lax.axis_index("expert")
    half = lax.axis_index("dp")
    other = 1 - core

    def expert_at(k):
        return lax.rem(me + k, ne)

    def wait(ref, sem):
        pltpu.make_async_copy(ref, ref, sem).wait()

    def to_core(src, dst, send, recv):
        return pltpu.make_async_remote_copy(
            src_ref=src, dst_ref=dst, send_sem=send, recv_sem=recv,
            device_id={"section": other}, device_id_type=MESH,
        )

    def to_dp(src, dst, send, recv):
        return pltpu.make_async_remote_copy(
            src_ref=src, dst_ref=dst, send_sem=send, recv_sem=recv,
            device_id={"dp": 1 - half}, device_id_type=MESH,
        )

    barrier = pltpu.get_barrier_semaphore()

    def greet(k, _):
        pl.semaphore_signal(barrier, inc=1, device_id={"expert": expert_at(k)}, device_id_type=MESH)
        return _

    pl.semaphore_signal(barrier, inc=1, device_id={"section": other}, device_id_type=MESH)
    pl.semaphore_signal(barrier, inc=1, device_id={"dp": 1 - half}, device_id_type=MESH)
    lax.fori_loop(1, ne, greet, 0)

    which = iota((8, KP), 0)
    for m in range(2):
        meta_m[m] = jnp.where(which < 2, -64.0, 0.0)
        meta_m[m, 0:2, 0:seq] = routes[m].astype(F32)
        meta_m[m, 2:4, 0:seq] = keep[m].astype(F32)
    small_m[0:ne] = router[...]
    small_m[ne:ne + 1] = gain_one[...]
    small_m[ne + 1:ne + 2] = gain_two[...]
    small_m[ne + 2:ne + 8] = jnp.zeros((6, width), F32)
    held = [
        (meta_m.at[core], meta_m.at[other], meta_s),
        (small_m, small_m, small_s),
        (w_qkv.at[0], w_qkv.at[0], wqkv_s),
        (w_out.at[0], w_out.at[0], wout_s),
        (w_in.at[0, 0], w_in.at[0, 0], win_s),
        (w_back.at[0, 0], w_back.at[0, 0], wback_s),
    ]
    for i, (mine, _, dst) in enumerate(held):
        pltpu.make_async_copy(mine, dst.at[core], wsem.at[core, i]).start()

    for ref in (nrm, qs, att, sec):
        for b in range(2):
            ref[b, t_rows:KP, :] = jnp.zeros((KP - t_rows, ref.shape[2]), BF)
    for ref in (dbr, dqkv):
        ref[t_rows:KP, :] = jnp.zeros((KP - t_rows, ref.shape[1]), BF)
    for b in range(2):
        vs[b, t_rows:KP, :] = jnp.zeros((KP - t_rows, width), BF)
    smt[...] = jnp.zeros(smt.shape, F32)
    row, col = iota((3 * gt, gm), 0), iota((3 * gt, gm), 1)
    chunk = (row >= gt).astype(jnp.int32) + (row >= 2 * gt).astype(jnp.int32)
    n = row - chunk * gt
    bits = gs.bit_length() - 1
    s_s[...] = one_hot(((col >> 4) == (n & (gs - 1))) & ((col & 15) == 4 * chunk + (n >> bits)))

    pl.semaphore_wait(barrier, ne + 1)
    for i, (_, theirs, dst) in enumerate(held):
        to_core(theirs, dst.at[core], wsend.at[i], wsem.at[core, i]).start()

    def weight(b, i):
        wait(held[i][2].at[b], wsem.at[b, i])

    def send(phase, g, rows_of, back):
        main, tail = rows_of[0:gm], rows_of[gm:gr]
        at = pl.ds(g * gs, gs)
        slot = ORDER.index(phase) % 4
        if g == (GROUPS - 1 if back else 0) and ORDER.index(phase) >= 4:
            wait(tx.at[slot, pl.ds(1, ne - 1)], a2s.at[slot])
        for c in range(3):
            tx[slot, at, 16 * c:16 * c + 16, :] = main[:, LANE * c:LANE * c + LANE].reshape(gs, 16, LANE)
        stack = jnp.concatenate([tail[:, LANE * c:LANE * c + LANE] for c in range(3)], axis=0)
        tx[slot, at, 48:64, :] = mm_tn(s_s[...], stack).astype(BF).reshape(gs, 16, LANE)
        own = 0 if back else ne - 1
        first = 1 if back and g == 0 else g * gs
        last = ne - 1 if not back and g == GROUPS - 1 else g * gs + gs

        def step(i, _):
            pltpu.make_async_remote_copy(
                src_ref=tx.at[slot, i], dst_ref=rx.at[phase, ne - 1 - i],
                send_sem=a2s.at[slot], recv_sem=a2r.at[phase, GROUPS - 1 - g],
                device_id={"expert": expert_at(i if back else i + 1)}, device_id_type=MESH,
            ).start()
            return _

        lax.fori_loop(first, last, step, 0)
        if g * gs <= own < g * gs + gs:
            pltpu.make_async_copy(
                tx.at[slot, own], rx.at[phase, ne - 1 - own], a2r.at[phase, GROUPS - 1 - g]
            ).start()

    def receive(phase, g, out, start):
        at = pl.ds(g * gs, gs)
        wait(rx.at[phase, at], a2r.at[phase, g])
        for c in range(3):
            out[start:start + gm, LANE * c:LANE * c + LANE] = rx[phase, at, 16 * c:16 * c + 16, :].reshape(gm, LANE)
        tail = mm(s_s[...], rx[phase, at, 48:64, :].reshape(gm, LANE)).astype(BF)
        for c in range(3):
            out[start + gm:start + gr, LANE * c:LANE * c + LANE] = tail[c * gt:c * gt + gt]

    def place_of(rank, slot):
        group = jnp.floor(rank * (1.0 / gs))
        within = rank - group * gs
        return group * gr + jnp.where(slot < MAIN, within * MAIN + slot, gm + (slot - MAIN) * gs + within)

    def route(b):
        data = meta_s[b]
        mef = (me + 1).astype(F32)
        chosen, keeps = [data[0:1], data[1:2]], [data[2:3], data[3:4]]
        rank = [r - mef for r in chosen]
        rank = [jnp.where(r < 0.0, r + ne, r) for r in rank]
        lanes = iota((ne, KP), 0).astype(F32)
        marks = [one_hot(lanes == r, F32) for r in rank]
        earlier = one_hot(iota((KP, KP), 0) < iota((KP, KP), 1))
        before = mm((marks[0] + marks[1]).astype(BF), earlier)
        slot = [jnp.sum(before * m, axis=0, keepdims=True) for m in marks]
        spot = iota((rows, KP), 0).astype(F32)
        for k in range(2):
            dt[b, :, KP * k:KP * k + KP] = one_hot(spot == place_of(rank[k], slot[k]))
        which = iota((8, KP), 0)
        lines = jnp.zeros((8, KP), F32)
        for i, line in enumerate((*rank, *slot, *keeps, *chosen)):
            lines = jnp.where(which == i, line, lines)
        same = one_hot(iota((t_rows, KP), 0) == iota((t_rows, KP), 1))
        cols = mm_nt(same, lines.astype(BF))
        cols_s[b] = cols
        spot = iota((t_rows, rows), 1).astype(F32)
        for k in range(2):
            dd[b, k] = one_hot(spot == place_of(cols[:, k:k + 1], cols[:, 2 + k:3 + k]))

    def chosen_marks(b):
        lanes = iota((t_rows, ne), 1).astype(F32)
        return [one_hot(lanes == cols_s[b, :, 6 + k:7 + k], F32) * cols_s[b, :, 4 + k:5 + k] for k in range(2)]

    def head_masks():
        lanes = iota((1, PAIR), 1)
        return [one_hot(lanes < HEAD), one_hot(lanes >= HEAD)]

    def forward_dense(b, x):
        hat, rstd = norm_parts(x)
        xh1[b], rs1[b] = hat, rstd
        normed = (hat * small_s[b, ne:ne + 1, :]).astype(BF)
        nrm[b, 0:t_rows, :] = normed
        weight(b, 2)
        qs[b, 0:t_rows, :] = mm(normed, wqkv_s[b]).astype(BF)
        masks = head_masks()
        real = iota((t_rows, KP), 1) < seq
        for p in range(HEADS // 2):
            at = PAIR * p
            query, key = qs[b, 0:t_rows, at:at + PAIR], qs[b, :, width + at:width + at + PAIR]
            value = qs[b, :, 2 * width + at:2 * width + at + PAIR]
            out = jnp.zeros((t_rows, PAIR), F32)
            for h in range(2):
                scores = mm_nt(query * masks[h], key) * SCALE
                scores = jnp.where(real, scores, -1e30)
                e = jnp.exp(scores - jnp.max(scores, axis=-1, keepdims=True))
                probs = e * (1.0 / jnp.sum(e, axis=-1, keepdims=True))
                ps[b, 2 * p + h] = probs
                out = out + mm(probs.astype(BF), value * masks[h])
            att[b, 0:t_rows, at:at + PAIR] = out.astype(BF)
        weight(b, 3)
        mixed = x + mm(att[b, 0:t_rows, :], wout_s[b])
        mix[...] = mixed
        hat, rstd = norm_parts(mixed)
        xh2[b], rs2[b] = hat, rstd
        second = hat * small_s[b, ne + 1:ne + 2, :]
        sec[b, 0:t_rows, :] = second.astype(BF)
        for g in range(GROUPS):
            at = slice(g * gr, g * gr + gr)
            send(4 * b, g, mm(dt[b, at, 0:KP] + dt[b, at, KP:2 * KP], sec[b]).astype(BF), False)
        logits = mm_nt(second, small_s[b, 0:ne, :], HIGHEST)
        e = jnp.exp(logits - jnp.max(logits, axis=-1, keepdims=True))
        probs = e / jnp.sum(e, axis=-1, keepdims=True)
        prb[b] = probs
        for k, marks in enumerate(chosen_marks(b)):
            gate_s[b, k] = jnp.sum(marks * probs, axis=-1, keepdims=True)

    steps = ff // CHUNK

    def chunk_at(i):
        return pl.ds(pl.multiple_of(i * CHUNK, CHUNK), CHUNK)

    def forward_expert(b):
        weight(b, 4)
        weight(b, 5)
        for h in range(GROUPS - 1, -1, -1):
            at = slice(h * gr, h * gr + gr)
            receive(4 * b, h, in_s.at[b, 0], h * gr)
            hidden = mm(in_s[b, 0, at, :], win_s[b])
            active = (hidden * phi_of(hidden)).astype(BF)
            ac_s[b, 0, at, :] = active
            send(4 * b + 1, h, mm(active, wback_s[b]).astype(BF), True)

    def slopes(b, side):
        def step(n, _):
            at = pl.ds(pl.multiple_of(lax.rem(n, GROUPS) * gr, 16), gr)
            cols = chunk_at(lax.div(n, GROUPS))
            hidden = mm(in_s[b, side, at, :], win_s[b, :, cols])
            phi = phi_of(hidden)
            dg_s[b, side, at, cols] = slope_of(hidden, phi).astype(BF)
            if side == 1:
                ac_s[b, side, at, cols] = (hidden * phi).astype(BF)
            return _

        lax.fori_loop(0, GROUPS * steps, step, 0)

    def rows_to_dp(ref, b, i):
        to_dp(ref.at[b, 0], ref.at[b, 1], dps.at[i], dpr_sem.at[i]).start()

    def rows_from_dp(ref, b, i):
        wait(ref.at[b, 1], dpr_sem.at[i])

    def forward_combine(b):
        for g in range(GROUPS):
            receive(4 * b + 1, g, ret, g * gr)
        rows_to_dp(in_s, b, b)
        y = mix[...]
        for k in range(2):
            picked = mm(dd[b, k], ret[...])
            pk[b, k] = picked.astype(BF)
            y = y + gate_s[b, k] * picked
        low = y.astype(BF)
        ya[b] = low
        return low.astype(F32)

    def backward_start(b, dy):
        d_probs = jnp.zeros((t_rows, ne), F32)
        for k, marks in enumerate(chosen_marks(b)):
            d_gate = jnp.sum(dy * pk[b, k].astype(F32), axis=-1, keepdims=True)
            d_probs = d_probs + marks * d_gate
            vs[k, 0:t_rows, :] = (gate_s[b, k] * dy).astype(BF)
        for g in range(GROUPS):
            at = slice(g * gr, g * gr + gr)
            part = mm(dt[b, at, 0:KP], vs[0]) + mm(dt[b, at, KP:2 * KP], vs[1])
            send(4 * b + 2, g, part.astype(BF), False)
        probs = prb[b]
        d_logits = probs * (d_probs - jnp.sum(probs * d_probs, axis=-1, keepdims=True))
        dsr[...] = mm(d_logits, small_s[b, 0:ne, :], HIGHEST)
        return mm_tn(d_logits, xh2[b] * small_s[b, ne + 1:ne + 2, :], HIGHEST)

    def hidden_grad(b, side, at, cols):
        slope = dg_s[b, side, at, cols].astype(F32)
        d_hidden = (mm_nt(dp_s[b, side, at, :], wback_s[b, cols, :]) * slope).astype(BF)
        dg_s[b, side, at, cols] = d_hidden
        return d_hidden

    def backward_expert(b):
        for h in range(GROUPS - 1, -1, -1):
            at = slice(h * gr, h * gr + gr)
            receive(4 * b + 2, h, dp_s.at[b, 0], h * gr)
            d_hidden = hidden_grad(b, 0, at, slice(None))
            send(4 * b + 3, h, mm_nt(d_hidden, win_s[b]).astype(BF), True)

    def far_hidden_grad(b):
        rows_from_dp(dp_s, b, 2 + b)

        def step(n, _):
            hidden_grad(b, 1, pl.ds(pl.multiple_of(lax.rem(n, GROUPS) * gr, 16), gr), chunk_at(lax.div(n, GROUPS)))
            return _

        lax.fori_loop(0, GROUPS * steps, step, 0)

    def in_grads(b):
        def step(i, _):
            cols = chunk_at(i)
            grad = mm_tn(in_s[b].reshape(2 * rows, width), dg_s[b, :, :, cols].reshape(2 * rows, CHUNK))
            wtx_i[:, cols] = grad.astype(BF)
            return _

        lax.fori_loop(0, steps, step, 0)

        @pl.when(core != b)
        def _():
            to_core(wtx_i, wrc_i, cxs.at[0], cxr.at[0]).start()

    def back_grads(b):
        def step(i, _):
            cols = chunk_at(i)
            grad = mm_tn(ac_s[b, :, :, cols].reshape(2 * rows, CHUNK), dp_s[b].reshape(2 * rows, width))
            wtx_b[cols, :] = grad.astype(BF)
            return _

        lax.fori_loop(0, steps, step, 0)

        @pl.when(core != b)
        def _():
            to_core(wtx_b, wrc_b, cxs.at[1], cxr.at[1]).start()

    def expert_out(b):
        @pl.when(core == b)
        def _():
            wait(wrc_i, cxr.at[0])
            wtx_i[...] = (wtx_i[...].astype(F32) + wrc_i[...].astype(F32)).astype(BF)
            pltpu.make_async_copy(wtx_i, wi_o, osem.at[0]).start()
            wait(wrc_b, cxr.at[1])
            wtx_b[...] = (wtx_b[...].astype(F32) + wrc_b[...].astype(F32)).astype(BF)
            pltpu.make_async_copy(wtx_b, wb_o, osem.at[1]).start()

    def in_sent(b):
        @pl.when(core != b)
        def _():
            wait(wtx_i, cxs.at[0])

        @pl.when(core == b)
        def _():
            wait(wi_o, osem.at[0])

    def back_sent(b):
        @pl.when(core != b)
        def _():
            wait(wtx_b, cxs.at[1])

        @pl.when(core == b)
        def _():
            wait(wb_o, osem.at[1])

    def dense_sent(b):
        @pl.when(core != b)
        def _():
            wait(den, cxs.at[2])

        @pl.when(core == b)
        def _():
            wait(den.at[pl.ds(1, ne - 1)], rss)

    def keep_dense(q, grad):
        for c in range(3):
            part = grad[:, LANE * c:LANE * c + LANE].astype(BF)
            den[q * per:q * per + per, piece * c:piece * c + piece, :] = part.reshape(per, piece, LANE)

    def backward_attention(b, dy):
        for g in range(GROUPS):
            receive(4 * b + 3, g, ret, g * gr)
        rows_to_dp(dp_s, b, 2 + b)
        d_second = mm(dd[b, 0] + dd[b, 1], ret[...]) + dsr[...]
        hat2 = xh2[b]
        d_gain_two = jnp.sum(d_second * hat2, axis=0, keepdims=True)
        d_mixed = dy + norm_back(d_second * small_s[b, ne + 1:ne + 2, :], hat2, rs2[b])
        dmx[...] = d_mixed
        d_branch = d_mixed.astype(BF)
        dbr[0:t_rows, :] = d_branch
        d_att = mm_nt(d_branch, wout_s[b]).astype(BF)
        masks = head_masks()
        for p in range(HEADS // 2):
            at = PAIR * p
            query, key = qs[b, 0:t_rows, at:at + PAIR], qs[b, :, width + at:width + at + PAIR]
            value = qs[b, :, 2 * width + at:2 * width + at + PAIR]
            d_query = jnp.zeros((t_rows, PAIR), F32)
            d_key = jnp.zeros((KP, PAIR), F32)
            d_value = jnp.zeros((KP, PAIR), F32)
            for h in range(2):
                d_out = d_att[:, at:at + PAIR] * masks[h]
                probs = ps[b, 2 * p + h]
                d_value = d_value + mm_tn(probs.astype(BF), d_out)
                d_probs = mm_nt(d_out, value)
                inner = jnp.sum(probs * d_probs, axis=-1, keepdims=True)
                d_scores = (probs * (d_probs - inner)).astype(BF)
                d_query = d_query + mm(d_scores, key * masks[h])
                d_key = d_key + mm_tn(d_scores, query * masks[h])
            dqkv[0:t_rows, at:at + PAIR] = (d_query * SCALE).astype(BF)
            dqkv[:, width + at:width + at + PAIR] = (d_key * SCALE).astype(BF)
            dqkv[:, 2 * width + at:2 * width + at + PAIR] = d_value.astype(BF)
        return d_gain_two

    def backward_input(b):
        d_normed = mm_nt(dqkv[0:t_rows, :], wqkv_s[b])
        hat1 = xh1[b]
        d_gain_one = jnp.sum(d_normed * hat1, axis=0, keepdims=True)
        return dmx[...] + norm_back(d_normed * small_s[b, ne:ne + 1, :], hat1, rs1[b]), d_gain_one

    def dense_grads(b):
        keep_dense(3, mm_tn(att[b], dbr[...]))
        for q in range(3):
            keep_dense(q, mm_tn(nrm[b], dqkv[:, width * q:width * q + width]))

    def dense_send(b, d_router, d_gain_one, d_gain_two):
        for c in range(3):
            at = LANE * c
            smt[:, c, :] = d_router[:, at:at + LANE]
            smt[c, 3:4, :] = d_gain_one[:, at:at + LANE]
            smt[c, 4:5, :] = d_gain_two[:, at:at + LANE]
        den[:, 3 * piece:3 * piece + 16, :] = smt[...].astype(BF)

        @pl.when(core != b)
        def _():
            to_core(den, den_rc, cxs.at[2], cxr.at[2]).start()

    def dense_scatter(b):
        @pl.when(core == b)
        def _():
            wait(den_rc, cxr.at[2])

            def step(k, _):
                to = expert_at(k)
                den[to] = (den[to].astype(F32) + den_rc[to].astype(F32)).astype(BF)
                pltpu.make_async_remote_copy(
                    src_ref=den.at[to], dst_ref=rs_rx.at[ne - k], send_sem=rss, recv_sem=rsr,
                    device_id={"expert": to}, device_id_type=MESH,
                ).start()
                return _

            lax.fori_loop(1, ne, step, 0)
            dpt[...] = den[me].astype(F32) + den_rc[me].astype(F32)

    def dense_reduce(b):
        @pl.when(core == b)
        def _():
            wait(rs_rx.at[pl.ds(1, ne - 1)], rsr)

            def step(k, total):
                return total + rs_rx[k].astype(F32)

            dpt[...] = lax.fori_loop(1, ne, step, dpt[...])
            to_dp(dpt, dpr, dps.at[4], dpr_sem.at[4]).start()

    def dense_gather(b):
        @pl.when(core == b)
        def _():
            wait(dpr, dpr_sem.at[4])
            agt[...] = (dpt[...] + dpr[...]).astype(BF)

            def step(k, _):
                to = expert_at(k)
                pltpu.make_async_remote_copy(
                    src_ref=agt, dst_ref=ag_rx.at[ne - k], send_sem=ags, recv_sem=agr,
                    device_id={"expert": to}, device_id_type=MESH,
                ).start()
                return _

            lax.fori_loop(1, ne, step, 0)

    def dense_finish(b):
        @pl.when(core == b)
        def _():
            wait(ag_rx.at[pl.ds(1, ne - 1)], agr)
            ag_rx[0] = agt[...]

            def step(k, _):
                to = expert_at(k)
                smfin[to] = ag_rx[k, 3 * piece:3 * piece + 16, :]
                block, at = lax.div(to, per), pl.multiple_of(lax.rem(to, per) * piece, 16)
                for c in range(3):
                    dfin_q[block, pl.ds(at, piece), LANE * c:LANE * c + LANE] = ag_rx[k, piece * c:piece * c + piece, :]
                return _

            lax.fori_loop(0, ne, step, 0)
            for q in range(3):
                pltpu.make_async_copy(dfin_q.at[q], qkv_o.at[:, pl.ds(width * q, width)], osem.at[6 + q]).start()
            pltpu.make_async_copy(dfin_q.at[3], out_o, osem.at[9]).start()
            pltpu.make_async_copy(smfin, sm_o, osem.at[10]).start()
            wait(ag_rx.at[pl.ds(1, ne - 1)], ags)
            wait(dpt, dps.at[4])

    x = images[...].astype(F32)
    weight(0, 0)
    weight(0, 1)
    route(0)
    for b in range(2):
        forward_dense(b, x)
        if b == 0:
            weight(1, 0)
            weight(1, 1)
            route(1)
        else:
            rows_from_dp(in_s, 0, 0)
            slopes(0, 1)
        forward_expert(b)
        slopes(b, 0)
        x = forward_combine(b)
    to_core(ya.at[other], ya_rx, acs, acr).start()
    dy = cot[...].astype(F32)
    d_router = backward_start(1, dy)
    rows_from_dp(in_s, 1, 1)
    slopes(1, 1)
    backward_expert(1)
    d_gain_two = backward_attention(1, dy)
    dx, d_gain_one = backward_input(1)
    dy = dx.astype(BF).astype(F32)
    gx[1] = dy
    d_router_0 = backward_start(0, dy)
    dense_grads(1)
    dense_send(1, d_router, d_gain_one, d_gain_two)
    backward_expert(0)
    dense_scatter(1)
    far_hidden_grad(1)
    in_grads(1)
    d_gain_two = backward_attention(0, dy)
    dense_sent(1)
    dense_grads(0)
    dx, d_gain_one = backward_input(0)
    dense_send(0, d_router_0, d_gain_one, d_gain_two)
    gx[0] = dx
    to_core(gx.at[other], gx_rx, igs, igr).start()
    dense_reduce(1)
    dense_scatter(0)
    back_grads(1)
    expert_out(1)
    dense_gather(1)
    far_hidden_grad(0)
    in_sent(1)
    in_grads(0)
    dense_reduce(0)
    back_sent(1)
    back_grads(0)
    dense_finish(1)
    dense_gather(0)
    wait(ya_rx, acr)
    pltpu.make_async_copy(ya.at[core], act_o.at[core], osem.at[2]).start()
    pltpu.make_async_copy(ya_rx, act_o.at[other], osem.at[3]).start()
    wait(gx_rx, igr)
    pltpu.make_async_copy(gx.at[core], ig_o.at[core], osem.at[4]).start()
    pltpu.make_async_copy(gx_rx, ig_o.at[other], osem.at[5]).start()
    expert_out(0)
    dense_finish(0)
    in_sent(0)
    back_sent(0)
    dense_sent(0)
    for i, (_, theirs, _dst) in enumerate(held):
        wait(theirs, wsend.at[i])
    for slot in range(4):
        wait(tx.at[slot, pl.ds(1, ne - 1)], a2s.at[slot])
    for b in range(2):
        wait(in_s.at[b, 0], dps.at[b])
        wait(dp_s.at[b, 0], dps.at[2 + b])
    wait(ya.at[other], acs)
    wait(gx.at[other], igs)
    for i, ref in enumerate((act_o.at[0], act_o.at[0], ig_o.at[0], ig_o.at[0])):
        wait(ref, osem.at[2 + i])
    for q in range(3):
        wait(dfin_q.at[q], osem.at[6 + q])
    wait(out_o, osem.at[9])
    wait(sm_o, osem.at[10])


def body(images_in, cotangent, gain_one, w_qkv, w_out, gain_two, w_router, w_in, w_back, routes, keep):
    micro, _, seq, width = images_in.shape
    ne = lax.axis_size("expert")
    ff = w_in.shape[3]
    t_rows = -(-seq // 16) * 16
    rows = ne * (MAIN + TAIL)
    gs = ne // GROUPS
    piece = 4 * width // ne
    core = lax.axis_index("section")

    def own(tokens):
        mine = lax.dynamic_index_in_dim(tokens[:, 0], core, 0, keepdims=False)
        return jnp.pad(mine, ((0, t_rows - seq), (0, 0)))

    vmem, anywhere = pl.BlockSpec(memory_space=pltpu.VMEM), pl.BlockSpec(memory_space=pl.ANY)
    dma = pltpu.SemaphoreType.DMA

    def v(*shape, dtype=BF):
        return pltpu.VMEM(shape, dtype)

    t, r, w, deep = t_rows, rows, width, 3 * piece + 16
    scratch = [
        v(2, 8, KP, dtype=F32), v(2, 8, KP, dtype=F32), v(ne + 8, w, dtype=F32), v(2, ne + 8, w, dtype=F32),
        v(2, w, 3 * w), v(2, w, w), v(2, w, ff), v(2, ff, w),
        v(3 * gs * TAIL, gs * MAIN),
        v(2, t, w, dtype=F32), v(2, t, 1, dtype=F32), v(2, t, w, dtype=F32), v(2, t, 1, dtype=F32),
        v(2, KP, w), v(2, KP, 3 * w), v(2, HEADS, t, KP, dtype=F32), v(2, KP, w),
        v(t, w, dtype=F32), v(2, KP, w), v(2, t, ne, dtype=F32),
        v(2, t, 8, dtype=F32), v(2, 2, t, 1, dtype=F32), v(2, 2, t, w), v(2, 2, t, r), v(2, r, 2 * KP),
        v(4, ne, 64, LANE), v(8, ne, 64, LANE), v(2, 2, r, w), v(2, 2, r, ff), v(2, 2, r, ff), v(2, 2, r, w),
        v(r, w),
        v(2, KP, w), v(t, w, dtype=F32), v(KP, w), v(KP, 3 * w), v(t, w, dtype=F32),
        v(2, t, w), v(t, w), v(2, t, w, dtype=F32), v(t, w, dtype=F32),
        v(w, ff), v(ff, w), v(w, ff), v(ff, w),
        v(ne, deep, LANE), v(ne, deep, LANE), v(ne, 16, LANE, dtype=F32), v(ne, deep, LANE),
        v(deep, LANE, dtype=F32), v(deep, LANE, dtype=F32), v(deep, LANE), v(ne, deep, LANE),
        v(4, w, w), v(ne, 16, LANE),
        dma((2, 6)), dma((6,)), dma((4,)), dma((8, GROUPS)), dma((3,)), dma((3,)), dma((5,)), dma((5,)),
        dma, dma, dma, dma, dma, dma, dma, dma, dma((11,)),
    ]
    shapes = [
        ((2, t, w), BF), ((2, t, w), F32), ((w, 3 * w), BF), ((w, w), BF), ((ne, 16, LANE), BF),
        ((w, ff), BF), ((ff, w), BF),
    ]
    act, grad, d_qkv, d_out, sm, d_in, d_back = pl.pallas_call(
        lambda *refs: kernel((seq, width, ff, ne), *refs),
        out_shape=[jax.ShapeDtypeStruct(s, d) for s, d in shapes],
        in_specs=[vmem] * 7 + [anywhere] * 4,
        out_specs=[anywhere] * 7,
        scratch_shapes=scratch,
        compiler_params=pltpu.CompilerParams(
            collective_id=0, has_side_effects=True, vmem_limit_bytes=62 * 2**20
        ),
        name="blocks",
    )(
        own(images_in), own(cotangent),
        jnp.swapaxes(routes[0, :, 0], 1, 2), jnp.swapaxes(keep[0, :, 0], 1, 2),
        gain_one, gain_two, w_router[0].T, w_qkv, w_out, w_in, w_back,
    )
    sm = sm.astype(F32)
    return (
        act[None, :, None, :seq],
        grad[None, :, None, :seq],
        sm[0:3, 3].reshape(1, width),
        d_qkv.astype(F32)[None],
        d_out.astype(F32)[None],
        sm[0:3, 4].reshape(1, width),
        sm[:, 0:3].reshape(ne, width).T[None],
        d_in.astype(F32)[None, None],
        d_back.astype(F32)[None, None],
    )


def solution(mesh):
    spread = ("expert", "dp")
    tokens = P(None, spread, None, None)
    per_block = P("section", None, spread, None, None)
    vector, matrix, experts = P("section", None), P("section", None, None), P("section", "expert", None, None)
    return jax.shard_map(
        body,
        mesh=mesh,
        in_specs=(
            tokens, tokens, vector, matrix, matrix, vector, matrix, experts, experts, per_block, per_block,
        ),
        out_specs=(
            per_block, per_block, vector, matrix, matrix, vector, matrix, experts, experts,
        ),
        check_vma=False,
    )
```

```python
import math

import jax
import jax.numpy as jnp
from jax import lax
from jax.experimental import pallas as pl
from jax.experimental.pallas import tpu as pltpu
from jax.sharding import PartitionSpec as P

HEADS = 6
HEAD = 64
PAIR = 2 * HEAD
SCALE = HEAD ** (-0.5)
EPSILON = 1e-06
HIGHEST = lax.Precision.HIGHEST
BF = jnp.bfloat16
F32 = jnp.float32
LANE = 128
MAIN = 16
TAIL = 4
KP = 256
CHUNK = 512
ORDER = (0, 1, 4, 5, 6, 7, 2, 3)
SPLIT = 7
GROUPS = 4
MESH = pl.DeviceIdType.MESH


def mm(a, b, precision=None):
    return lax.dot_general(a, b, (((1,), (0,)), ((), ())), precision=precision, preferred_element_type=F32)


def mm_nt(a, b, precision=None):
    return lax.dot_general(a, b, (((1,), (1,)), ((), ())), precision=precision, preferred_element_type=F32)


def mm_tn(a, b, precision=None):
    return lax.dot_general(a, b, (((0,), (0,)), ((), ())), precision=precision, preferred_element_type=F32)


def iota(shape, dim):
    return lax.broadcasted_iota(jnp.int32, shape, dim)


def one_hot(hit, dtype=BF):
    return jnp.where(hit, 1.0, 0.0).astype(dtype)


def phi_of(h):
    return 0.5 * lax.erf(h * (0.5**0.5)) + 0.5


def slope_of(h, phi):
    return phi + h * (jnp.exp(h * h * -0.5) * (1.0 / math.sqrt(2.0 * math.pi)))


def norm_parts(x):
    cen = x - jnp.mean(x, axis=-1, keepdims=True)
    rstd = lax.rsqrt(jnp.mean(cen * cen, axis=-1, keepdims=True) + EPSILON)
    return cen * rstd, rstd


def norm_back(d_hat, hat, rstd):
    return rstd * (
        d_hat
        - jnp.mean(d_hat, axis=-1, keepdims=True)
        - hat * jnp.mean(d_hat * hat, axis=-1, keepdims=True)
    )


def kernel(dims, *refs):
    seq, width, ff, ne = dims
    t_rows = -(-seq // 16) * 16
    gs = ne // GROUPS
    gm, gt = gs * MAIN, gs * TAIL
    gr = gm + gt
    rows = ne * (MAIN + TAIL)
    piece = width * 4 // ne
    per = ne // 4
    (
        images, cot, routes, keep, gain_one, gain_two, router, w_qkv, w_out, w_in, w_back,
        act_o, ig_o, qkv_o, out_o, sm_o, wi_o, wb_o,
        meta_m, meta_s, small_m, small_s, wqkv_s, wout_s, win_s, wback_s,
        s_s, xh1, rs1, xh2, rs2, nrm, qs, ps, att, mix, sec, prb, cols_s, gate_s, pk, dd, dt,
        tx, rx, in_s, ac_s, dg_s, dp_s, ret, vs, dsr, dbr, dqkv, dmx, ya, ya_rx, gx, gx_rx,
        wtx_i, wtx_b, wrc_i, wrc_b,
        den, den_rc, smt, rs_rx, dpt, dpr, agt, ag_rx, dfin_q, smfin,
        wsem, wsend, a2s, a2r, cxs, cxr, dps, dpr_sem, rss, rsr, ags, agr, acs, acr, igs, igr, osem,
    ) = refs
    core = lax.axis_index("section")
    me = lax.axis_index("expert")
    half = lax.axis_index("dp")
    other = 1 - core

    def expert_at(k):
        return lax.rem(me + k, ne)

    def wait(ref, sem):
        pltpu.make_async_copy(ref, ref, sem).wait()

    def to_core(src, dst, send, recv):
        return pltpu.make_async_remote_copy(
            src_ref=src, dst_ref=dst, send_sem=send, recv_sem=recv,
            device_id={"section": other}, device_id_type=MESH,
        )

    def to_dp(src, dst, send, recv):
        return pltpu.make_async_remote_copy(
            src_ref=src, dst_ref=dst, send_sem=send, recv_sem=recv,
            device_id={"dp": 1 - half}, device_id_type=MESH,
        )

    barrier = pltpu.get_barrier_semaphore()

    def greet(k, _):
        pl.semaphore_signal(barrier, inc=1, device_id={"expert": expert_at(k)}, device_id_type=MESH)
        return _

    pl.semaphore_signal(barrier, inc=1, device_id={"section": other}, device_id_type=MESH)
    pl.semaphore_signal(barrier, inc=1, device_id={"dp": 1 - half}, device_id_type=MESH)
    lax.fori_loop(1, ne, greet, 0)

    which = iota((8, KP), 0)
    for m in range(2):
        meta_m[m] = jnp.where(which < 2, -64.0, 0.0)
        meta_m[m, 0:2, 0:seq] = routes[m].astype(F32)
        meta_m[m, 2:4, 0:seq] = keep[m].astype(F32)
    small_m[0:ne] = router[...]
    small_m[ne:ne + 1] = gain_one[...]
    small_m[ne + 1:ne + 2] = gain_two[...]
    small_m[ne + 2:ne + 8] = jnp.zeros((6, width), F32)
    held = [
        (meta_m.at[core], meta_m.at[other], meta_s),
        (small_m, small_m, small_s),
        (w_qkv.at[0], w_qkv.at[0], wqkv_s),
        (w_out.at[0], w_out.at[0], wout_s),
        (w_in.at[0, 0], w_in.at[0, 0], win_s),
        (w_back.at[0, 0], w_back.at[0, 0], wback_s),
    ]
    for i, (mine, _, dst) in enumerate(held):
        pltpu.make_async_copy(mine, dst.at[core], wsem.at[core, i]).start()

    for ref in (nrm, qs, att, sec):
        for b in range(2):
            ref[b, t_rows:KP, :] = jnp.zeros((KP - t_rows, ref.shape[2]), BF)
    for ref in (dbr, dqkv):
        ref[t_rows:KP, :] = jnp.zeros((KP - t_rows, ref.shape[1]), BF)
    for b in range(2):
        vs[b, t_rows:KP, :] = jnp.zeros((KP - t_rows, width), BF)
    smt[...] = jnp.zeros(smt.shape, F32)
    row, col = iota((3 * gt, gm), 0), iota((3 * gt, gm), 1)
    chunk = (row >= gt).astype(jnp.int32) + (row >= 2 * gt).astype(jnp.int32)
    n = row - chunk * gt
    bits = gs.bit_length() - 1
    s_s[...] = one_hot(((col >> 4) == (n & (gs - 1))) & ((col & 15) == 4 * chunk + (n >> bits)))

    pl.semaphore_wait(barrier, ne + 1)
    for i, (_, theirs, dst) in enumerate(held):
        to_core(theirs, dst.at[core], wsend.at[i], wsem.at[core, i]).start()

    def weight(b, i):
        wait(held[i][2].at[b], wsem.at[b, i])

    def send(phase, g, rows_of, back):
        main, tail = rows_of[0:gm], rows_of[gm:gr]
        at = pl.ds(g * gs, gs)
        slot = ORDER.index(phase) % 4
        if g == (GROUPS - 1 if back else 0) and ORDER.index(phase) >= 4:
            wait(tx.at[slot, pl.ds(1, ne - 1)], a2s.at[slot])
        for c in range(3):
            tx[slot, at, 16 * c:16 * c + 16, :] = main[:, LANE * c:LANE * c + LANE].reshape(gs, 16, LANE)
        stack = jnp.concatenate([tail[:, LANE * c:LANE * c + LANE] for c in range(3)], axis=0)
        tx[slot, at, 48:64, :] = mm_tn(s_s[...], stack).astype(BF).reshape(gs, 16, LANE)
        own = 0 if back else ne - 1
        first = 1 if back and g == 0 else g * gs
        last = ne - 1 if not back and g == GROUPS - 1 else g * gs + gs

        def step(i, _):
            pltpu.make_async_remote_copy(
                src_ref=tx.at[slot, i], dst_ref=rx.at[phase, ne - 1 - i],
                send_sem=a2s.at[slot], recv_sem=a2r.at[phase, GROUPS - 1 - g],
                device_id={"expert": expert_at(i if back else i + 1)}, device_id_type=MESH,
            ).start()
            return _

        lax.fori_loop(first, last, step, 0)
        if g * gs <= own < g * gs + gs:
            pltpu.make_async_copy(
                tx.at[slot, own], rx.at[phase, ne - 1 - own], a2r.at[phase, GROUPS - 1 - g]
            ).start()

    def receive(phase, g, out, start):
        at = pl.ds(g * gs, gs)
        wait(rx.at[phase, at], a2r.at[phase, g])
        for c in range(3):
            out[start:start + gm, LANE * c:LANE * c + LANE] = rx[phase, at, 16 * c:16 * c + 16, :].reshape(gm, LANE)
        tail = mm(s_s[...], rx[phase, at, 48:64, :].reshape(gm, LANE)).astype(BF)
        for c in range(3):
            out[start + gm:start + gr, LANE * c:LANE * c + LANE] = tail[c * gt:c * gt + gt]

    def place_of(rank, slot):
        group = jnp.floor(rank * (1.0 / gs))
        within = rank - group * gs
        return group * gr + jnp.where(slot < MAIN, within * MAIN + slot, gm + (slot - MAIN) * gs + within)

    def route(b):
        data = meta_s[b]
        mef = (me + 1).astype(F32)
        chosen, keeps = [data[0:1], data[1:2]], [data[2:3], data[3:4]]
        rank = [r - mef for r in chosen]
        rank = [jnp.where(r < 0.0, r + ne, r) for r in rank]
        lanes = iota((ne, KP), 0).astype(F32)
        marks = [one_hot(lanes == r, F32) for r in rank]
        earlier = one_hot(iota((KP, KP), 0) < iota((KP, KP), 1))
        before = mm((marks[0] + marks[1]).astype(BF), earlier)
        slot = [jnp.sum(before * m, axis=0, keepdims=True) for m in marks]
        spot = iota((rows, KP), 0).astype(F32)
        for k in range(2):
            dt[b, :, KP * k:KP * k + KP] = one_hot(spot == place_of(rank[k], slot[k]))
        which = iota((8, KP), 0)
        lines = jnp.zeros((8, KP), F32)
        for i, line in enumerate((*rank, *slot, *keeps, *chosen)):
            lines = jnp.where(which == i, line, lines)
        same = one_hot(iota((t_rows, KP), 0) == iota((t_rows, KP), 1))
        cols = mm_nt(same, lines.astype(BF))
        cols_s[b] = cols
        spot = iota((t_rows, rows), 1).astype(F32)
        for k in range(2):
            dd[b, k] = one_hot(spot == place_of(cols[:, k:k + 1], cols[:, 2 + k:3 + k]))

    def chosen_marks(b):
        lanes = iota((t_rows, ne), 1).astype(F32)
        return [one_hot(lanes == cols_s[b, :, 6 + k:7 + k], F32) * cols_s[b, :, 4 + k:5 + k] for k in range(2)]

    def head_masks():
        lanes = iota((1, PAIR), 1)
        return [one_hot(lanes < HEAD), one_hot(lanes >= HEAD)]

    def forward_dense(b, x):
        hat, rstd = norm_parts(x)
        xh1[b], rs1[b] = hat, rstd
        normed = (hat * small_s[b, ne:ne + 1, :]).astype(BF)
        nrm[b, 0:t_rows, :] = normed
        weight(b, 2)
        qs[b, 0:t_rows, :] = mm(normed, wqkv_s[b]).astype(BF)
        masks = head_masks()
        real = iota((t_rows, KP), 1) < seq
        for p in range(HEADS // 2):
            at = PAIR * p
            query, key = qs[b, 0:t_rows, at:at + PAIR], qs[b, :, width + at:width + at + PAIR]
            value = qs[b, :, 2 * width + at:2 * width + at + PAIR]
            out = jnp.zeros((t_rows, PAIR), F32)
            for h in range(2):
                scores = mm_nt(query * masks[h], key) * SCALE
                scores = jnp.where(real, scores, -1e30)
                e = jnp.exp(scores - jnp.max(scores, axis=-1, keepdims=True))
                probs = e * (1.0 / jnp.sum(e, axis=-1, keepdims=True))
                ps[b, 2 * p + h] = probs
                out = out + mm(probs.astype(BF), value * masks[h])
            att[b, 0:t_rows, at:at + PAIR] = out.astype(BF)
        weight(b, 3)
        mixed = x + mm(att[b, 0:t_rows, :], wout_s[b])
        mix[...] = mixed
        hat, rstd = norm_parts(mixed)
        xh2[b], rs2[b] = hat, rstd
        second = hat * small_s[b, ne + 1:ne + 2, :]
        sec[b, 0:t_rows, :] = second.astype(BF)
        for g in range(GROUPS):
            at = slice(g * gr, g * gr + gr)
            send(4 * b, g, mm(dt[b, at, 0:KP] + dt[b, at, KP:2 * KP], sec[b]).astype(BF), False)
        logits = mm_nt(second, small_s[b, 0:ne, :], HIGHEST)
        e = jnp.exp(logits - jnp.max(logits, axis=-1, keepdims=True))
        probs = e / jnp.sum(e, axis=-1, keepdims=True)
        prb[b] = probs
        for k, marks in enumerate(chosen_marks(b)):
            gate_s[b, k] = jnp.sum(marks * probs, axis=-1, keepdims=True)

    steps = ff // CHUNK

    def chunk_at(i):
        return pl.ds(pl.multiple_of(i * CHUNK, CHUNK), CHUNK)

    def forward_expert(b):
        weight(b, 4)
        weight(b, 5)
        for h in range(GROUPS - 1, -1, -1):
            at = slice(h * gr, h * gr + gr)
            receive(4 * b, h, in_s.at[b, 0], h * gr)
            hidden = mm(in_s[b, 0, at, :], win_s[b])
            active = (hidden * phi_of(hidden)).astype(BF)
            ac_s[b, 0, at, :] = active
            send(4 * b + 1, h, mm(active, wback_s[b]).astype(BF), True)

    def slopes(b, side):
        def step(i, _):
            cols = chunk_at(i)
            hidden = mm(in_s[b, side], win_s[b, :, cols])
            phi = phi_of(hidden)
            dg_s[b, side, :, cols] = slope_of(hidden, phi).astype(BF)
            if side == 1:
                ac_s[b, side, :, cols] = (hidden * phi).astype(BF)
            return _

        lax.fori_loop(0, steps, step, 0)

    def rows_to_dp(ref, b, i, low, high):
        at = pl.ds(low * (rows // 10), (high - low) * (rows // 10))
        to_dp(ref.at[b, 0, at], ref.at[b, 1, at], dps.at[i], dpr_sem.at[i]).start()

    def rows_from_dp(ref, b, i):
        wait(ref.at[b, 1], dpr_sem.at[i])

    def forward_combine(b):
        for g in range(GROUPS):
            receive(4 * b + 1, g, ret, g * gr)
        y = mix[...]
        for k in range(2):
            picked = mm(dd[b, k], ret[...])
            pk[b, k] = picked.astype(BF)
            y = y + gate_s[b, k] * picked
        low = y.astype(BF)
        ya[b] = low
        return low.astype(F32)

    def backward_start(b, dy):
        d_probs = jnp.zeros((t_rows, ne), F32)
        for k, marks in enumerate(chosen_marks(b)):
            d_gate = jnp.sum(dy * pk[b, k].astype(F32), axis=-1, keepdims=True)
            d_probs = d_probs + marks * d_gate
            vs[k, 0:t_rows, :] = (gate_s[b, k] * dy).astype(BF)
        for g in range(GROUPS):
            at = slice(g * gr, g * gr + gr)
            part = mm(dt[b, at, 0:KP], vs[0]) + mm(dt[b, at, KP:2 * KP], vs[1])
            send(4 * b + 2, g, part.astype(BF), False)
        probs = prb[b]
        d_logits = probs * (d_probs - jnp.sum(probs * d_probs, axis=-1, keepdims=True))
        dsr[...] = mm(d_logits, small_s[b, 0:ne, :], HIGHEST)
        return mm_tn(d_logits, xh2[b] * small_s[b, ne + 1:ne + 2, :], HIGHEST)

    def hidden_grad(b, side, at, cols):
        slope = dg_s[b, side, at, cols].astype(F32)
        d_hidden = (mm_nt(dp_s[b, side, at, :], wback_s[b, cols, :]) * slope).astype(BF)
        dg_s[b, side, at, cols] = d_hidden
        return d_hidden

    def backward_expert(b):
        for h in range(GROUPS - 1, -1, -1):
            at = slice(h * gr, h * gr + gr)
            receive(4 * b + 2, h, dp_s.at[b, 0], h * gr)
            d_hidden = hidden_grad(b, 0, at, slice(None))
            send(4 * b + 3, h, mm_nt(d_hidden, win_s[b]).astype(BF), True)

    def far_hidden_grad(b):
        rows_from_dp(dp_s, b, 2 + b)

        def step(i, _):
            hidden_grad(b, 1, slice(None), chunk_at(i))
            return _

        lax.fori_loop(0, steps, step, 0)

    def in_grads(b):
        def step(i, _):
            cols = chunk_at(i)
            grad = mm_tn(in_s[b].reshape(2 * rows, width), dg_s[b, :, :, cols].reshape(2 * rows, CHUNK))
            wtx_i[:, cols] = grad.astype(BF)
            return _

        lax.fori_loop(0, steps, step, 0)

        @pl.when(core != b)
        def _():
            to_core(wtx_i, wrc_i, cxs.at[0], cxr.at[0]).start()

    def back_grads(b):
        def step(i, _):
            cols = chunk_at(i)
            grad = mm_tn(ac_s[b, :, :, cols].reshape(2 * rows, CHUNK), dp_s[b].reshape(2 * rows, width))
            wtx_b[cols, :] = grad.astype(BF)
            return _

        lax.fori_loop(0, steps, step, 0)

        @pl.when(core != b)
        def _():
            to_core(wtx_b, wrc_b, cxs.at[1], cxr.at[1]).start()

    def expert_out(b):
        @pl.when(core == b)
        def _():
            wait(wrc_i, cxr.at[0])
            wtx_i[...] = (wtx_i[...].astype(F32) + wrc_i[...].astype(F32)).astype(BF)
            pltpu.make_async_copy(wtx_i, wi_o, osem.at[0]).start()
            wait(wrc_b, cxr.at[1])
            wtx_b[...] = (wtx_b[...].astype(F32) + wrc_b[...].astype(F32)).astype(BF)
            pltpu.make_async_copy(wtx_b, wb_o, osem.at[1]).start()

    def in_sent(b):
        @pl.when(core != b)
        def _():
            wait(wtx_i, cxs.at[0])

        @pl.when(core == b)
        def _():
            wait(wi_o, osem.at[0])

    def back_sent(b):
        @pl.when(core != b)
        def _():
            wait(wtx_b, cxs.at[1])

        @pl.when(core == b)
        def _():
            wait(wb_o, osem.at[1])

    def dense_part(b, q, grad, smalls=()):
        at = slice(q * per, q * per + per)
        for c in range(3):
            part = grad[:, LANE * c:LANE * c + LANE].astype(BF)
            den[b, at, piece * c:piece * c + piece, :] = part.reshape(per, piece, LANE)
        for first, small in smalls:
            for c in range(3):
                smt[0, first + c:first + c + 1, :] = small[:, LANE * c:LANE * c + LANE]
        den[b, at, 3 * piece:3 * piece + 16, :] = smt[at].astype(BF)

        @pl.when(core != b)
        def _():
            to_core(den.at[b, at], den_rc.at[at], cxs.at[2 + q], cxr.at[2 + q]).start()

    def dense_out(b, d_router):
        for c in range(3):
            smt[:, c, :] = d_router[:, LANE * c:LANE * c + LANE]
        dense_part(b, 3, mm_tn(att[b], dbr[...]))

    def dense_qkv(b, q, smalls=()):
        dense_part(b, q, mm_tn(nrm[b], dqkv[:, width * q:width * q + width]), smalls)

    def dense_sent(b):
        @pl.when(core != b)
        def _():
            for q in range(4):
                at = slice(q * per, q * per + per)
                wait(den.at[b, at], cxs.at[2 + q])

        @pl.when(core == b)
        def _():
            wait(den.at[b, pl.ds(1, ne - 1)], rss)

    def backward_attention(b, dy, early=None):
        for g in range(GROUPS):
            receive(4 * b + 3, g, ret, g * gr)
        d_second = mm(dd[b, 0] + dd[b, 1], ret[...]) + dsr[...]
        hat2 = xh2[b]
        d_gain_two = jnp.sum(d_second * hat2, axis=0, keepdims=True)
        d_mixed = dy + norm_back(d_second * small_s[b, ne + 1:ne + 2, :], hat2, rs2[b])
        dmx[...] = d_mixed
        d_branch = d_mixed.astype(BF)
        dbr[0:t_rows, :] = d_branch
        d_att = mm_nt(d_branch, wout_s[b]).astype(BF)
        if early is not None:
            early()
        masks = head_masks()
        for p in range(HEADS // 2):
            at = PAIR * p
            query, key = qs[b, 0:t_rows, at:at + PAIR], qs[b, :, width + at:width + at + PAIR]
            value = qs[b, :, 2 * width + at:2 * width + at + PAIR]
            d_query = jnp.zeros((t_rows, PAIR), F32)
            d_key = jnp.zeros((KP, PAIR), F32)
            d_value = jnp.zeros((KP, PAIR), F32)
            for h in range(2):
                d_out = d_att[:, at:at + PAIR] * masks[h]
                probs = ps[b, 2 * p + h]
                d_value = d_value + mm_tn(probs.astype(BF), d_out)
                d_probs = mm_nt(d_out, value)
                inner = jnp.sum(probs * d_probs, axis=-1, keepdims=True)
                d_scores = (probs * (d_probs - inner)).astype(BF)
                d_query = d_query + mm(d_scores, key * masks[h])
                d_key = d_key + mm_tn(d_scores, query * masks[h])
            dqkv[0:t_rows, at:at + PAIR] = (d_query * SCALE).astype(BF)
            dqkv[:, width + at:width + at + PAIR] = (d_key * SCALE).astype(BF)
            dqkv[:, 2 * width + at:2 * width + at + PAIR] = d_value.astype(BF)
        return d_gain_two

    def backward_input(b):
        d_normed = mm_nt(dqkv[0:t_rows, :], wqkv_s[b])
        hat1 = xh1[b]
        d_gain_one = jnp.sum(d_normed * hat1, axis=0, keepdims=True)
        return dmx[...] + norm_back(d_normed * small_s[b, ne:ne + 1, :], hat1, rs1[b]), d_gain_one

    def dense_scatter(b, q):
        @pl.when(core == b)
        def _():
            at = slice(q * per, q * per + per)
            wait(den_rc.at[at], cxr.at[2 + q])

            def step(to, carry):
                total = den[b, to].astype(F32) + den_rc[to].astype(F32)

                @pl.when(to == me)
                def _():
                    dpt[...] = total

                @pl.when(to != me)
                def _():
                    den[b, to] = total.astype(BF)
                    pltpu.make_async_remote_copy(
                        src_ref=den.at[b, to], dst_ref=rs_rx.at[lax.rem(me - to + ne, ne)], send_sem=rss, recv_sem=rsr,
                        device_id={"expert": to}, device_id_type=MESH,
                    ).start()

                return carry

            lax.fori_loop(q * per, q * per + per, step, 0)

    def dense_reduce(b):
        @pl.when(core == b)
        def _():
            wait(rs_rx.at[pl.ds(1, ne - 1)], rsr)

            def step(k, total):
                return total + rs_rx[k].astype(F32)

            dpt[...] = lax.fori_loop(1, ne, step, dpt[...])
            to_dp(dpt, dpr, dps.at[4], dpr_sem.at[4]).start()

    def dense_gather(b):
        @pl.when(core == b)
        def _():
            wait(dpr, dpr_sem.at[4])
            agt[...] = (dpt[...] + dpr[...]).astype(BF)

            def step(k, _):
                to = expert_at(k)
                pltpu.make_async_remote_copy(
                    src_ref=agt, dst_ref=ag_rx.at[ne - k], send_sem=ags, recv_sem=agr,
                    device_id={"expert": to}, device_id_type=MESH,
                ).start()
                return _

            lax.fori_loop(1, ne, step, 0)

    def dense_finish(b):
        @pl.when(core == b)
        def _():
            wait(ag_rx.at[pl.ds(1, ne - 1)], agr)
            ag_rx[0] = agt[...]

            def step(k, _):
                to = expert_at(k)
                smfin[to] = ag_rx[k, 3 * piece:3 * piece + 16, :]
                block, at = lax.div(to, per), pl.multiple_of(lax.rem(to, per) * piece, 16)
                for c in range(3):
                    dfin_q[block, pl.ds(at, piece), LANE * c:LANE * c + LANE] = ag_rx[k, piece * c:piece * c + piece, :]
                return _

            lax.fori_loop(0, ne, step, 0)
            for q in range(3):
                pltpu.make_async_copy(dfin_q.at[q], qkv_o.at[:, pl.ds(width * q, width)], osem.at[6 + q]).start()
            pltpu.make_async_copy(dfin_q.at[3], out_o, osem.at[9]).start()
            pltpu.make_async_copy(smfin, sm_o, osem.at[10]).start()
            wait(ag_rx.at[pl.ds(1, ne - 1)], ags)
            wait(dpt, dps.at[4])

    x = images[...].astype(F32)
    weight(0, 0)
    weight(0, 1)
    route(0)
    forward_dense(0, x)
    weight(1, 0)
    weight(1, 1)
    route(1)
    forward_expert(0)
    rows_to_dp(in_s, 0, 0, 0, SPLIT)
    slopes(0, 0)
    x = forward_combine(0)
    forward_dense(1, x)
    rows_to_dp(in_s, 0, 0, SPLIT, 10)
    forward_expert(1)
    rows_to_dp(in_s, 1, 1, 0, SPLIT)
    slopes(1, 0)
    forward_combine(1)
    dy = cot[...].astype(F32)
    d_router = backward_start(1, dy)
    rows_to_dp(in_s, 1, 1, SPLIT, 10)
    to_core(ya.at[other], ya_rx, acs, acr).start()
    rows_from_dp(in_s, 0, 0)
    slopes(0, 1)
    backward_expert(1)
    rows_to_dp(dp_s, 1, 3, 0, SPLIT)
    rows_from_dp(in_s, 1, 1)
    slopes(1, 1)
    d_gain_two = backward_attention(1, dy)
    dx, d_gain_one = backward_input(1)
    dy = dx.astype(BF).astype(F32)
    gx[1] = dy
    d_router_0 = backward_start(0, dy)
    rows_to_dp(dp_s, 1, 3, SPLIT, 10)
    dense_out(1, d_router)
    dense_qkv(1, 2)
    dense_qkv(1, 1)
    dense_qkv(1, 0, ((3, d_gain_one), (6, d_gain_two)))
    backward_expert(0)
    for q in (3, 2, 1, 0):
        dense_scatter(1, q)
    rows_to_dp(dp_s, 0, 2, 0, 10)
    far_hidden_grad(1)
    in_grads(1)
    d_gain_two = backward_attention(0, dy, lambda: dense_out(0, d_router_0))
    dense_qkv(0, 2)
    dense_scatter(0, 3)
    dense_qkv(0, 1)
    dx, d_gain_one = backward_input(0)
    dense_qkv(0, 0, ((3, d_gain_one), (6, d_gain_two)))
    dense_reduce(1)
    dense_scatter(0, 2)
    dense_scatter(0, 1)
    dense_scatter(0, 0)
    gx[0] = dx
    to_core(gx.at[other], gx_rx, igs, igr).start()
    dense_gather(1)
    back_grads(1)
    expert_out(1)
    far_hidden_grad(0)
    in_sent(1)
    in_grads(0)
    dense_reduce(0)
    dense_gather(0)
    back_sent(1)
    back_grads(0)
    dense_finish(1)
    wait(ya_rx, acr)
    act_o[core] = ya[core, 0:seq, :]
    act_o[other] = ya_rx[0:seq, :]
    wait(gx_rx, igr)
    ig_o[core] = gx[core, 0:seq, :]
    ig_o[other] = gx_rx[0:seq, :]
    expert_out(0)
    dense_finish(0)
    in_sent(0)
    back_sent(0)
    dense_sent(0)
    dense_sent(1)
    for i, (_, theirs, _dst) in enumerate(held):
        wait(theirs, wsend.at[i])
    for slot in range(4):
        wait(tx.at[slot, pl.ds(1, ne - 1)], a2s.at[slot])
    for b in range(2):
        wait(in_s.at[b, 0], dps.at[b])
        wait(dp_s.at[b, 0], dps.at[2 + b])
    wait(ya.at[other], acs)
    wait(gx.at[other], igs)
    for q in range(3):
        wait(dfin_q.at[q], osem.at[6 + q])
    wait(out_o, osem.at[9])
    wait(sm_o, osem.at[10])


def widen(*refs):
    for source, out in zip(refs[:4], refs[4:]):
        out[...] = source[...].astype(F32)


def body(images_in, cotangent, gain_one, w_qkv, w_out, gain_two, w_router, w_in, w_back, routes, keep):
    micro, _, seq, width = images_in.shape
    ne = lax.axis_size("expert")
    ff = w_in.shape[3]
    t_rows = -(-seq // 16) * 16
    rows = ne * (MAIN + TAIL)
    gs = ne // GROUPS
    piece = 4 * width // ne
    core = lax.axis_index("section")

    def own(tokens):
        mine = lax.dynamic_index_in_dim(tokens[:, 0], core, 0, keepdims=False)
        return jnp.pad(mine, ((0, t_rows - seq), (0, 0)))

    vmem, anywhere = pl.BlockSpec(memory_space=pltpu.VMEM), pl.BlockSpec(memory_space=pl.ANY)
    dma = pltpu.SemaphoreType.DMA

    def v(*shape, dtype=BF):
        return pltpu.VMEM(shape, dtype)

    t, r, w, deep = t_rows, rows, width, 3 * piece + 16
    scratch = [
        v(2, 8, KP, dtype=F32), v(2, 8, KP, dtype=F32), v(ne + 8, w, dtype=F32), v(2, ne + 8, w, dtype=F32),
        v(2, w, 3 * w), v(2, w, w), v(2, w, ff), v(2, ff, w),
        v(3 * gs * TAIL, gs * MAIN),
        v(2, t, w, dtype=F32), v(2, t, 1, dtype=F32), v(2, t, w, dtype=F32), v(2, t, 1, dtype=F32),
        v(2, KP, w), v(2, KP, 3 * w), v(2, HEADS, t, KP, dtype=F32), v(2, KP, w),
        v(t, w, dtype=F32), v(2, KP, w), v(2, t, ne, dtype=F32),
        v(2, t, 8, dtype=F32), v(2, 2, t, 1, dtype=F32), v(2, 2, t, w), v(2, 2, t, r), v(2, r, 2 * KP),
        v(4, ne, 64, LANE), v(8, ne, 64, LANE), v(2, 2, r, w), v(2, 2, r, ff), v(2, 2, r, ff), v(2, 2, r, w),
        v(r, w),
        v(2, KP, w), v(t, w, dtype=F32), v(KP, w), v(KP, 3 * w), v(t, w, dtype=F32),
        v(2, t, w), v(t, w), v(2, t, w, dtype=F32), v(t, w, dtype=F32),
        v(w, ff), v(ff, w), v(w, ff), v(ff, w),
        v(2, ne, deep, LANE), v(ne, deep, LANE), v(ne, 16, LANE, dtype=F32), v(ne, deep, LANE),
        v(deep, LANE, dtype=F32), v(deep, LANE, dtype=F32), v(deep, LANE), v(ne, deep, LANE),
        v(4, w, w), v(ne, 16, LANE),
        dma((2, 6)), dma((6,)), dma((4,)), dma((8, GROUPS)), dma((6,)), dma((6,)), dma((5,)), dma((5,)),
        dma, dma, dma, dma, dma, dma, dma, dma, dma((11,)),
    ]
    shapes = [
        ((2, seq, w), BF), ((2, seq, w), F32), ((w, 3 * w), BF), ((w, w), BF), ((ne, 16, LANE), BF),
        ((w, ff), BF), ((ff, w), BF),
    ]
    act, grad, d_qkv, d_out, sm, d_in, d_back = pl.pallas_call(
        lambda *refs: kernel((seq, width, ff, ne), *refs),
        out_shape=[jax.ShapeDtypeStruct(s, d) for s, d in shapes],
        in_specs=[vmem] * 7 + [anywhere] * 4,
        out_specs=[vmem] * 2 + [anywhere] * 5,
        scratch_shapes=scratch,
        compiler_params=pltpu.CompilerParams(
            collective_id=0, has_side_effects=True, vmem_limit_bytes=62 * 2**20
        ),
        name="blocks",
    )(
        own(images_in), own(cotangent),
        jnp.swapaxes(routes[0, :, 0], 1, 2), jnp.swapaxes(keep[0, :, 0], 1, 2),
        gain_one, gain_two, w_router[0].T, w_qkv, w_out, w_in, w_back,
    )
    steps = 8
    weights = ((d_qkv, (w // steps, 3 * w)), (d_out, (w // steps, w)), (d_in, (w // steps, ff)), (d_back, (ff // steps, w)))
    specs = [pl.BlockSpec(block, lambda i: (i, 0)) for _, block in weights]
    d_qkv, d_out, d_in, d_back = pl.pallas_call(
        widen,
        grid=(steps,),
        out_shape=[jax.ShapeDtypeStruct(value.shape, F32) for value, _ in weights],
        in_specs=specs,
        out_specs=specs,
        name="widen",
    )(*[value for value, _ in weights])
    sm = sm.astype(F32)
    return (
        act[None, :, None],
        grad[None, :, None],
        sm[0, 3:6].reshape(1, width),
        d_qkv[None],
        d_out[None],
        sm[0, 6:9].reshape(1, width),
        sm[:, 0:3].reshape(ne, width).T[None],
        d_in[None, None],
        d_back[None, None],
    )


def solution(mesh):
    spread = ("expert", "dp")
    tokens = P(None, spread, None, None)
    per_block = P("section", None, spread, None, None)
    vector, matrix, experts = P("section", None), P("section", None, None), P("section", "expert", None, None)
    return jax.shard_map(
        body,
        mesh=mesh,
        in_specs=(
            tokens, tokens, vector, matrix, matrix, vector, matrix, experts, experts, per_block, per_block,
        ),
        out_specs=(
            per_block, per_block, vector, matrix, matrix, vector, matrix, experts, experts,
        ),
        check_vma=False,
    )
```

```python
import math

import jax
import jax.numpy as jnp
from jax import lax
from jax.experimental import pallas as pl
from jax.experimental.pallas import tpu as pltpu
from jax.sharding import PartitionSpec as P

HEADS = 6
HEAD = 64
PAIR = 2 * HEAD
SCALE = HEAD ** (-0.5)
EPSILON = 1e-06
HIGHEST = lax.Precision.HIGHEST
BF = jnp.bfloat16
F32 = jnp.float32
LANE = 128
MAIN = 16
TAIL = 4
KP = 256
CHUNK = 512
ORDER = (0, 1, 4, 5, 6, 7, 2, 3)
SPLIT = 7
GROUPS = 4
MESH = pl.DeviceIdType.MESH


def mm(a, b, precision=None):
    return lax.dot_general(a, b, (((1,), (0,)), ((), ())), precision=precision, preferred_element_type=F32)


def mm_nt(a, b, precision=None):
    return lax.dot_general(a, b, (((1,), (1,)), ((), ())), precision=precision, preferred_element_type=F32)


def mm_tn(a, b, precision=None):
    return lax.dot_general(a, b, (((0,), (0,)), ((), ())), precision=precision, preferred_element_type=F32)


def iota(shape, dim):
    return lax.broadcasted_iota(jnp.int32, shape, dim)


def one_hot(hit, dtype=BF):
    return jnp.where(hit, 1.0, 0.0).astype(dtype)


def phi_of(h):
    return 0.5 * lax.erf(h * (0.5**0.5)) + 0.5


def slope_of(h, phi):
    return phi + h * (jnp.exp(h * h * -0.5) * (1.0 / math.sqrt(2.0 * math.pi)))


def norm_parts(x):
    cen = x - jnp.mean(x, axis=-1, keepdims=True)
    rstd = lax.rsqrt(jnp.mean(cen * cen, axis=-1, keepdims=True) + EPSILON)
    return cen * rstd, rstd


def norm_back(d_hat, hat, rstd):
    return rstd * (
        d_hat
        - jnp.mean(d_hat, axis=-1, keepdims=True)
        - hat * jnp.mean(d_hat * hat, axis=-1, keepdims=True)
    )


def kernel(dims, *refs):
    seq, width, ff, ne = dims
    t_rows = -(-seq // 16) * 16
    gs = ne // GROUPS
    gm, gt = gs * MAIN, gs * TAIL
    gr = gm + gt
    rows = ne * (MAIN + TAIL)
    piece = width * 4 // ne
    per = ne // 4
    (
        images, cot, routes, keep, gain_one, gain_two, router, w_qkv, w_out, w_in, w_back,
        act_o, ig_o, router_o, gain1_o, gain2_o, qkv_o, out_o, wi_o, wb_o,
        meta_m, meta_s, small_m, small_s, wqkv_s, wout_s, win_s, wback_s,
        s_s, xh1, rs1, xh2, rs2, nrm, qs, ps, att, mix, sec, prb, cols_s, gate_s, pk, dd, dt,
        tx, rx, in_s, ac_s, dg_s, dp_s, ret, vs, dsr, dbr, dqkv, dmx, ya, ya_rx, gx, gx_rx,
        wtx_i, wtx_b, wrc_i, wrc_b,
        den, den_rc, smt, rs_rx, dpt, dpr, agt, ag_rx, dfin_q, smfin,
        wsem, wsend, a2s, a2r, cxs, cxr, dps, dpr_sem, rss, rsr, ags, agr, acs, acr, igs, igr, osem,
    ) = refs
    core = lax.axis_index("section")
    me = lax.axis_index("expert")
    half = lax.axis_index("dp")
    other = 1 - core

    def expert_at(k):
        return lax.rem(me + k, ne)

    def wait(ref, sem):
        pltpu.make_async_copy(ref, ref, sem).wait()

    def to_core(src, dst, send, recv):
        return pltpu.make_async_remote_copy(
            src_ref=src, dst_ref=dst, send_sem=send, recv_sem=recv,
            device_id={"section": other}, device_id_type=MESH,
        )

    def to_dp(src, dst, send, recv):
        return pltpu.make_async_remote_copy(
            src_ref=src, dst_ref=dst, send_sem=send, recv_sem=recv,
            device_id={"dp": 1 - half}, device_id_type=MESH,
        )

    barrier = pltpu.get_barrier_semaphore()

    def greet(k, _):
        pl.semaphore_signal(barrier, inc=1, device_id={"expert": expert_at(k)}, device_id_type=MESH)
        return _

    pl.semaphore_signal(barrier, inc=1, device_id={"section": other}, device_id_type=MESH)
    pl.semaphore_signal(barrier, inc=1, device_id={"dp": 1 - half}, device_id_type=MESH)
    lax.fori_loop(1, ne, greet, 0)

    which = iota((8, KP), 0)
    for m in range(2):
        meta_m[m] = jnp.where(which < 2, -64.0, 0.0)
        meta_m[m, 0:2, 0:seq] = routes[m].astype(F32)
        meta_m[m, 2:4, 0:seq] = keep[m].astype(F32)
    small_m[0:ne] = router[...]
    small_m[ne:ne + 1] = gain_one[...]
    small_m[ne + 1:ne + 2] = gain_two[...]
    small_m[ne + 2:ne + 8] = jnp.zeros((6, width), F32)
    held = [
        (meta_m.at[core], meta_m.at[other], meta_s),
        (small_m, small_m, small_s),
        (w_qkv.at[0], w_qkv.at[0], wqkv_s),
        (w_out.at[0], w_out.at[0], wout_s),
        (w_in.at[0, 0], w_in.at[0, 0], win_s),
        (w_back.at[0, 0], w_back.at[0, 0], wback_s),
    ]
    for i, (mine, _, dst) in enumerate(held):
        pltpu.make_async_copy(mine, dst.at[core], wsem.at[core, i]).start()

    for ref in (nrm, qs, att, sec):
        for b in range(2):
            ref[b, t_rows:KP, :] = jnp.zeros((KP - t_rows, ref.shape[2]), BF)
    for ref in (dbr, dqkv):
        ref[t_rows:KP, :] = jnp.zeros((KP - t_rows, ref.shape[1]), BF)
    for b in range(2):
        vs[b, t_rows:KP, :] = jnp.zeros((KP - t_rows, width), BF)
    smt[...] = jnp.zeros(smt.shape, F32)
    row, col = iota((3 * gt, gm), 0), iota((3 * gt, gm), 1)
    chunk = (row >= gt).astype(jnp.int32) + (row >= 2 * gt).astype(jnp.int32)
    n = row - chunk * gt
    bits = gs.bit_length() - 1
    s_s[...] = one_hot(((col >> 4) == (n & (gs - 1))) & ((col & 15) == 4 * chunk + (n >> bits)))

    pl.semaphore_wait(barrier, ne + 1)
    for i, (_, theirs, dst) in enumerate(held):
        to_core(theirs, dst.at[core], wsend.at[i], wsem.at[core, i]).start()

    def weight(b, i):
        wait(held[i][2].at[b], wsem.at[b, i])

    def send(phase, g, rows_of, back):
        main, tail = rows_of[0:gm], rows_of[gm:gr]
        at = pl.ds(g * gs, gs)
        slot = ORDER.index(phase) % 4
        if g == (GROUPS - 1 if back else 0) and ORDER.index(phase) >= 4:
            wait(tx.at[slot, pl.ds(1, ne - 1)], a2s.at[slot])
        for c in range(3):
            tx[slot, at, 16 * c:16 * c + 16, :] = main[:, LANE * c:LANE * c + LANE].reshape(gs, 16, LANE)
        stack = jnp.concatenate([tail[:, LANE * c:LANE * c + LANE] for c in range(3)], axis=0)
        tx[slot, at, 48:64, :] = mm_tn(s_s[...], stack).astype(BF).reshape(gs, 16, LANE)
        own = 0 if back else ne - 1
        first = 1 if back and g == 0 else g * gs
        last = ne - 1 if not back and g == GROUPS - 1 else g * gs + gs

        def step(i, _):
            pltpu.make_async_remote_copy(
                src_ref=tx.at[slot, i], dst_ref=rx.at[phase, ne - 1 - i],
                send_sem=a2s.at[slot], recv_sem=a2r.at[phase, GROUPS - 1 - g],
                device_id={"expert": expert_at(i if back else i + 1)}, device_id_type=MESH,
            ).start()
            return _

        lax.fori_loop(first, last, step, 0)
        if g * gs <= own < g * gs + gs:
            pltpu.make_async_copy(
                tx.at[slot, own], rx.at[phase, ne - 1 - own], a2r.at[phase, GROUPS - 1 - g]
            ).start()

    def receive(phase, g, out, start):
        at = pl.ds(g * gs, gs)
        wait(rx.at[phase, at], a2r.at[phase, g])
        for c in range(3):
            out[start:start + gm, LANE * c:LANE * c + LANE] = rx[phase, at, 16 * c:16 * c + 16, :].reshape(gm, LANE)
        tail = mm(s_s[...], rx[phase, at, 48:64, :].reshape(gm, LANE)).astype(BF)
        for c in range(3):
            out[start + gm:start + gr, LANE * c:LANE * c + LANE] = tail[c * gt:c * gt + gt]

    def place_of(rank, slot):
        group = jnp.floor(rank * (1.0 / gs))
        within = rank - group * gs
        return group * gr + jnp.where(slot < MAIN, within * MAIN + slot, gm + (slot - MAIN) * gs + within)

    def route(b):
        data = meta_s[b]
        mef = (me + 1).astype(F32)
        chosen, keeps = [data[0:1], data[1:2]], [data[2:3], data[3:4]]
        rank = [r - mef for r in chosen]
        rank = [jnp.where(r < 0.0, r + ne, r) for r in rank]
        lanes = iota((ne, KP), 0).astype(F32)
        marks = [one_hot(lanes == r, F32) for r in rank]
        earlier = one_hot(iota((KP, KP), 0) < iota((KP, KP), 1))
        before = mm((marks[0] + marks[1]).astype(BF), earlier)
        slot = [jnp.sum(before * m, axis=0, keepdims=True) for m in marks]
        spot = iota((rows, KP), 0).astype(F32)
        for k in range(2):
            dt[b, :, KP * k:KP * k + KP] = one_hot(spot == place_of(rank[k], slot[k]))
        which = iota((8, KP), 0)
        lines = jnp.zeros((8, KP), F32)
        for i, line in enumerate((*rank, *slot, *keeps, *chosen)):
            lines = jnp.where(which == i, line, lines)
        same = one_hot(iota((t_rows, KP), 0) == iota((t_rows, KP), 1))
        cols = mm_nt(same, lines.astype(BF))
        cols_s[b] = cols
        spot = iota((t_rows, rows), 1).astype(F32)
        for k in range(2):
            dd[b, k] = one_hot(spot == place_of(cols[:, k:k + 1], cols[:, 2 + k:3 + k]))

    def chosen_marks(b):
        lanes = iota((t_rows, ne), 1).astype(F32)
        return [one_hot(lanes == cols_s[b, :, 6 + k:7 + k], F32) * cols_s[b, :, 4 + k:5 + k] for k in range(2)]

    def head_masks():
        lanes = iota((1, PAIR), 1)
        return [one_hot(lanes < HEAD), one_hot(lanes >= HEAD)]

    def forward_dense(b, x):
        hat, rstd = norm_parts(x)
        xh1[b], rs1[b] = hat, rstd
        normed = (hat * small_s[b, ne:ne + 1, :]).astype(BF)
        nrm[b, 0:t_rows, :] = normed
        weight(b, 2)
        qs[b, 0:t_rows, :] = mm(normed, wqkv_s[b]).astype(BF)
        masks = head_masks()
        real = iota((t_rows, KP), 1) < seq
        for p in range(HEADS // 2):
            at = PAIR * p
            query, key = qs[b, 0:t_rows, at:at + PAIR], qs[b, :, width + at:width + at + PAIR]
            value = qs[b, :, 2 * width + at:2 * width + at + PAIR]
            out = jnp.zeros((t_rows, PAIR), F32)
            for h in range(2):
                scores = mm_nt(query * masks[h], key) * SCALE
                scores = jnp.where(real, scores, -1e30)
                e = jnp.exp(scores - jnp.max(scores, axis=-1, keepdims=True))
                probs = e * (1.0 / jnp.sum(e, axis=-1, keepdims=True))
                ps[b, 2 * p + h] = probs
                out = out + mm(probs.astype(BF), value * masks[h])
            att[b, 0:t_rows, at:at + PAIR] = out.astype(BF)
        weight(b, 3)
        mixed = x + mm(att[b, 0:t_rows, :], wout_s[b])
        mix[...] = mixed
        hat, rstd = norm_parts(mixed)
        xh2[b], rs2[b] = hat, rstd
        second = hat * small_s[b, ne + 1:ne + 2, :]
        sec[b, 0:t_rows, :] = second.astype(BF)
        for g in range(GROUPS):
            at = slice(g * gr, g * gr + gr)
            send(4 * b, g, mm(dt[b, at, 0:KP] + dt[b, at, KP:2 * KP], sec[b]).astype(BF), False)
        logits = mm_nt(second, small_s[b, 0:ne, :], HIGHEST)
        e = jnp.exp(logits - jnp.max(logits, axis=-1, keepdims=True))
        probs = e / jnp.sum(e, axis=-1, keepdims=True)
        prb[b] = probs
        for k, marks in enumerate(chosen_marks(b)):
            gate_s[b, k] = jnp.sum(marks * probs, axis=-1, keepdims=True)

    steps = ff // CHUNK

    def chunk_at(i):
        return pl.ds(pl.multiple_of(i * CHUNK, CHUNK), CHUNK)

    def forward_expert(b):
        weight(b, 4)
        weight(b, 5)
        for h in range(GROUPS - 1, -1, -1):
            at = slice(h * gr, h * gr + gr)
            receive(4 * b, h, in_s.at[b, 0], h * gr)
            hidden = mm(in_s[b, 0, at, :], win_s[b])
            active = (hidden * phi_of(hidden)).astype(BF)
            ac_s[b, 0, at, :] = active
            send(4 * b + 1, h, mm(active, wback_s[b]).astype(BF), True)

    def slopes(b, side):
        def step(i, _):
            cols = chunk_at(i)
            hidden = mm(in_s[b, side], win_s[b, :, cols])
            phi = phi_of(hidden)
            dg_s[b, side, :, cols] = slope_of(hidden, phi).astype(BF)
            if side == 1:
                ac_s[b, side, :, cols] = (hidden * phi).astype(BF)
            return _

        lax.fori_loop(0, steps, step, 0)

    def rows_to_dp(ref, b, i, low, high):
        at = pl.ds(low * (rows // 10), (high - low) * (rows // 10))
        to_dp(ref.at[b, 0, at], ref.at[b, 1, at], dps.at[i], dpr_sem.at[i]).start()

    def rows_from_dp(ref, b, i):
        wait(ref.at[b, 1], dpr_sem.at[i])

    def forward_combine(b):
        for g in range(GROUPS):
            receive(4 * b + 1, g, ret, g * gr)
        y = mix[...]
        for k in range(2):
            picked = mm(dd[b, k], ret[...])
            pk[b, k] = picked.astype(BF)
            y = y + gate_s[b, k] * picked
        low = y.astype(BF)
        ya[b] = low
        return low.astype(F32)

    def backward_start(b, dy):
        d_probs = jnp.zeros((t_rows, ne), F32)
        for k, marks in enumerate(chosen_marks(b)):
            d_gate = jnp.sum(dy * pk[b, k].astype(F32), axis=-1, keepdims=True)
            d_probs = d_probs + marks * d_gate
            vs[k, 0:t_rows, :] = (gate_s[b, k] * dy).astype(BF)
        for g in range(GROUPS):
            at = slice(g * gr, g * gr + gr)
            part = mm(dt[b, at, 0:KP], vs[0]) + mm(dt[b, at, KP:2 * KP], vs[1])
            send(4 * b + 2, g, part.astype(BF), False)
        probs = prb[b]
        d_logits = probs * (d_probs - jnp.sum(probs * d_probs, axis=-1, keepdims=True))
        dsr[...] = mm(d_logits, small_s[b, 0:ne, :], HIGHEST)
        return mm_tn(d_logits, xh2[b] * small_s[b, ne + 1:ne + 2, :], HIGHEST)

    def hidden_grad(b, side, at, cols):
        slope = dg_s[b, side, at, cols].astype(F32)
        d_hidden = (mm_nt(dp_s[b, side, at, :], wback_s[b, cols, :]) * slope).astype(BF)
        dg_s[b, side, at, cols] = d_hidden
        return d_hidden

    def backward_expert(b):
        for h in range(GROUPS - 1, -1, -1):
            at = slice(h * gr, h * gr + gr)
            receive(4 * b + 2, h, dp_s.at[b, 0], h * gr)
            d_hidden = hidden_grad(b, 0, at, slice(None))
            send(4 * b + 3, h, mm_nt(d_hidden, win_s[b]).astype(BF), True)

    def far_hidden_grad(b):
        rows_from_dp(dp_s, b, 2 + b)

        def step(i, _):
            hidden_grad(b, 1, slice(None), chunk_at(i))
            return _

        lax.fori_loop(0, steps, step, 0)

    def in_grads(b):
        def step(i, _):
            cols = chunk_at(i)
            grad = mm_tn(in_s[b].reshape(2 * rows, width), dg_s[b, :, :, cols].reshape(2 * rows, CHUNK))
            wtx_i[:, cols] = grad.astype(BF)
            return _

        lax.fori_loop(0, steps, step, 0)

        @pl.when(core != b)
        def _():
            to_core(wtx_i, wrc_i, cxs.at[0], cxr.at[0]).start()

    def back_grads(b):
        def step(i, _):
            cols = chunk_at(i)
            grad = mm_tn(ac_s[b, :, :, cols].reshape(2 * rows, CHUNK), dp_s[b].reshape(2 * rows, width))
            wtx_b[cols, :] = grad.astype(BF)
            return _

        lax.fori_loop(0, steps, step, 0)

        @pl.when(core != b)
        def _():
            to_core(wtx_b, wrc_b, cxs.at[1], cxr.at[1]).start()

    def expert_out(b):
        @pl.when(core == b)
        def _():
            wait(wrc_i, cxr.at[0])
            wtx_i[...] = (wtx_i[...].astype(F32) + wrc_i[...].astype(F32)).astype(BF)
            pltpu.make_async_copy(wtx_i, wi_o, osem.at[0]).start()
            wait(wrc_b, cxr.at[1])
            wtx_b[...] = (wtx_b[...].astype(F32) + wrc_b[...].astype(F32)).astype(BF)
            pltpu.make_async_copy(wtx_b, wb_o, osem.at[1]).start()

    def in_sent(b):
        @pl.when(core != b)
        def _():
            wait(wtx_i, cxs.at[0])

        @pl.when(core == b)
        def _():
            wait(wi_o, osem.at[0])

    def back_sent(b):
        @pl.when(core != b)
        def _():
            wait(wtx_b, cxs.at[1])

        @pl.when(core == b)
        def _():
            wait(wb_o, osem.at[1])

    def dense_part(b, q, grad, smalls=()):
        at = slice(q * per, q * per + per)
        for c in range(3):
            part = grad[:, LANE * c:LANE * c + LANE].astype(BF)
            den[b, at, piece * c:piece * c + piece, :] = part.reshape(per, piece, LANE)
        for first, small in smalls:
            for c in range(3):
                smt[0, first + c:first + c + 1, :] = small[:, LANE * c:LANE * c + LANE]
        den[b, at, 3 * piece:3 * piece + 16, :] = smt[at].astype(BF)

        @pl.when(core != b)
        def _():
            to_core(den.at[b, at], den_rc.at[at], cxs.at[2 + q], cxr.at[2 + q]).start()

    def dense_out(b, d_router):
        for c in range(3):
            smt[:, c, :] = d_router[:, LANE * c:LANE * c + LANE]
        dense_part(b, 3, mm_tn(att[b], dbr[...]))

    def dense_qkv(b, q, smalls=()):
        dense_part(b, q, mm_tn(nrm[b], dqkv[:, width * q:width * q + width]), smalls)

    def dense_sent(b):
        @pl.when(core != b)
        def _():
            for q in range(4):
                at = slice(q * per, q * per + per)
                wait(den.at[b, at], cxs.at[2 + q])

        @pl.when(core == b)
        def _():
            wait(den.at[b, pl.ds(1, ne - 1)], rss)

    def backward_attention(b, dy, early=None):
        for g in range(GROUPS):
            receive(4 * b + 3, g, ret, g * gr)
        d_second = mm(dd[b, 0] + dd[b, 1], ret[...]) + dsr[...]
        hat2 = xh2[b]
        d_gain_two = jnp.sum(d_second * hat2, axis=0, keepdims=True)
        d_mixed = dy + norm_back(d_second * small_s[b, ne + 1:ne + 2, :], hat2, rs2[b])
        dmx[...] = d_mixed
        d_branch = d_mixed.astype(BF)
        dbr[0:t_rows, :] = d_branch
        d_att = mm_nt(d_branch, wout_s[b]).astype(BF)
        if early is not None:
            early()
        masks = head_masks()
        for p in range(HEADS // 2):
            at = PAIR * p
            query, key = qs[b, 0:t_rows, at:at + PAIR], qs[b, :, width + at:width + at + PAIR]
            value = qs[b, :, 2 * width + at:2 * width + at + PAIR]
            d_query = jnp.zeros((t_rows, PAIR), F32)
            d_key = jnp.zeros((KP, PAIR), F32)
            d_value = jnp.zeros((KP, PAIR), F32)
            for h in range(2):
                d_out = d_att[:, at:at + PAIR] * masks[h]
                probs = ps[b, 2 * p + h]
                d_value = d_value + mm_tn(probs.astype(BF), d_out)
                d_probs = mm_nt(d_out, value)
                inner = jnp.sum(probs * d_probs, axis=-1, keepdims=True)
                d_scores = (probs * (d_probs - inner)).astype(BF)
                d_query = d_query + mm(d_scores, key * masks[h])
                d_key = d_key + mm_tn(d_scores, query * masks[h])
            dqkv[0:t_rows, at:at + PAIR] = (d_query * SCALE).astype(BF)
            dqkv[:, width + at:width + at + PAIR] = (d_key * SCALE).astype(BF)
            dqkv[:, 2 * width + at:2 * width + at + PAIR] = d_value.astype(BF)
        return d_gain_two

    def backward_input(b):
        d_normed = mm_nt(dqkv[0:t_rows, :], wqkv_s[b])
        hat1 = xh1[b]
        d_gain_one = jnp.sum(d_normed * hat1, axis=0, keepdims=True)
        return dmx[...] + norm_back(d_normed * small_s[b, ne:ne + 1, :], hat1, rs1[b]), d_gain_one

    def dense_scatter(b, q):
        @pl.when(core == b)
        def _():
            at = slice(q * per, q * per + per)
            wait(den_rc.at[at], cxr.at[2 + q])

            den[b, at] = (den[b, at].astype(F32) + den_rc[at].astype(F32)).astype(BF)

            def step(to, carry):
                @pl.when(to != me)
                def _():
                    pltpu.make_async_remote_copy(
                        src_ref=den.at[b, to], dst_ref=rs_rx.at[lax.rem(me - to + ne, ne)], send_sem=rss, recv_sem=rsr,
                        device_id={"expert": to}, device_id_type=MESH,
                    ).start()

                return carry

            lax.fori_loop(q * per, q * per + per, step, 0)

    def dense_reduce(b):
        @pl.when(core == b)
        def _():
            wait(rs_rx.at[pl.ds(1, ne - 1)], rsr)

            def step(k, total):
                return total + rs_rx[k].astype(F32)

            dpt[...] = lax.fori_loop(1, ne, step, den[b, me].astype(F32))
            to_dp(dpt, dpr, dps.at[4], dpr_sem.at[4]).start()

    def dense_gather(b):
        @pl.when(core == b)
        def _():
            wait(dpr, dpr_sem.at[4])
            agt[...] = (dpt[...] + dpr[...]).astype(BF)

            def step(k, _):
                to = expert_at(k)
                pltpu.make_async_remote_copy(
                    src_ref=agt, dst_ref=ag_rx.at[ne - k], send_sem=ags, recv_sem=agr,
                    device_id={"expert": to}, device_id_type=MESH,
                ).start()
                return _

            lax.fori_loop(1, ne, step, 0)

    def dense_finish(b):
        @pl.when(core == b)
        def _():
            wait(ag_rx.at[pl.ds(1, ne - 1)], agr)
            ag_rx[0] = agt[...]

            def step(k, _):
                to = expert_at(k)
                smfin[to] = ag_rx[k, 3 * piece:3 * piece + 16, :].astype(F32)
                block, at = lax.div(to, per), pl.multiple_of(lax.rem(to, per) * piece, 16)
                for c in range(3):
                    dfin_q[block, pl.ds(at, piece), LANE * c:LANE * c + LANE] = ag_rx[k, piece * c:piece * c + piece, :]
                return _

            lax.fori_loop(0, ne, step, 0)
            for q in range(3):
                pltpu.make_async_copy(dfin_q.at[q], qkv_o.at[:, pl.ds(width * q, width)], osem.at[6 + q]).start()
            pltpu.make_async_copy(dfin_q.at[3], out_o, osem.at[9]).start()
            for c in range(3):
                at = slice(LANE * c, LANE * c + LANE)
                router_o[:, at] = smfin[:, c, :]
                gain1_o[:, at] = smfin[0, 3 + c:4 + c, :]
                gain2_o[:, at] = smfin[0, 6 + c:7 + c, :]
            wait(ag_rx.at[pl.ds(1, ne - 1)], ags)
            wait(dpt, dps.at[4])

    x = images[...].astype(F32)
    weight(0, 0)
    weight(0, 1)
    route(0)
    forward_dense(0, x)
    weight(1, 0)
    weight(1, 1)
    route(1)
    forward_expert(0)
    rows_to_dp(in_s, 0, 0, 0, SPLIT)
    slopes(0, 0)
    x = forward_combine(0)
    forward_dense(1, x)
    rows_to_dp(in_s, 0, 0, SPLIT, 10)
    forward_expert(1)
    rows_to_dp(in_s, 1, 1, 0, SPLIT)
    slopes(1, 0)
    forward_combine(1)
    dy = cot[...].astype(F32)
    d_router = backward_start(1, dy)
    rows_to_dp(in_s, 1, 1, SPLIT, 10)
    to_core(ya.at[other], ya_rx, acs, acr).start()
    rows_from_dp(in_s, 0, 0)
    slopes(0, 1)
    backward_expert(1)
    rows_to_dp(dp_s, 1, 3, 0, SPLIT)
    rows_from_dp(in_s, 1, 1)
    slopes(1, 1)
    d_gain_two = backward_attention(1, dy)
    dx, d_gain_one = backward_input(1)
    dy = dx.astype(BF).astype(F32)
    gx[1] = dy
    d_router_0 = backward_start(0, dy)
    rows_to_dp(dp_s, 1, 3, SPLIT, 10)
    dense_out(1, d_router)
    dense_qkv(1, 2)
    dense_qkv(1, 1)
    dense_qkv(1, 0, ((3, d_gain_one), (6, d_gain_two)))
    backward_expert(0)
    for q in (3, 2, 1, 0):
        dense_scatter(1, q)
    rows_to_dp(dp_s, 0, 2, 0, 10)
    far_hidden_grad(1)
    in_grads(1)
    back_grads(1)
    d_gain_two = backward_attention(0, dy, lambda: dense_out(0, d_router_0))
    dense_qkv(0, 2)
    dense_scatter(0, 3)
    dense_qkv(0, 1)
    dx, d_gain_one = backward_input(0)
    dense_qkv(0, 0, ((3, d_gain_one), (6, d_gain_two)))
    dense_reduce(1)
    dense_scatter(0, 2)
    dense_scatter(0, 1)
    dense_scatter(0, 0)
    gx[0] = dx
    to_core(gx.at[other], gx_rx, igs, igr).start()
    expert_out(1)
    dense_gather(1)
    far_hidden_grad(0)
    in_sent(1)
    in_grads(0)
    dense_reduce(0)
    dense_gather(0)
    back_sent(1)
    back_grads(0)
    dense_finish(1)
    wait(ya_rx, acr)
    mine, theirs = ya[core].astype(F32), ya_rx[...].astype(F32)
    pair = [jnp.where(core == m, mine, theirs)[0:seq] for m in range(2)]
    act_o[...] = jnp.concatenate([p.reshape(seq, 1, width) for p in pair], axis=1).astype(BF)
    wait(gx_rx, igr)
    ig_o[pl.ds(core * seq, seq), 0, :] = gx[core, 0:seq, :]
    ig_o[pl.ds(other * seq, seq), 0, :] = gx_rx[0:seq, :]
    expert_out(0)
    dense_finish(0)
    in_sent(0)
    back_sent(0)
    dense_sent(0)
    dense_sent(1)
    for i, (_, theirs, _dst) in enumerate(held):
        wait(theirs, wsend.at[i])
    for slot in range(4):
        wait(tx.at[slot, pl.ds(1, ne - 1)], a2s.at[slot])
    for b in range(2):
        wait(in_s.at[b, 0], dps.at[b])
        wait(dp_s.at[b, 0], dps.at[2 + b])
    wait(ya.at[other], acs)
    wait(gx.at[other], igs)
    for q in range(3):
        wait(dfin_q.at[q], osem.at[6 + q])
    wait(out_o, osem.at[9])


def body(images_in, cotangent, gain_one, w_qkv, w_out, gain_two, w_router, w_in, w_back, routes, keep):
    micro, _, seq, width = images_in.shape
    ne = lax.axis_size("expert")
    ff = w_in.shape[3]
    t_rows = -(-seq // 16) * 16
    rows = ne * (MAIN + TAIL)
    gs = ne // GROUPS
    piece = 4 * width // ne
    core = lax.axis_index("section")

    def own(tokens):
        mine = lax.dynamic_index_in_dim(tokens[:, 0], core, 0, keepdims=False)
        return jnp.pad(mine, ((0, t_rows - seq), (0, 0)))

    vmem, anywhere = pl.BlockSpec(memory_space=pltpu.VMEM), pl.BlockSpec(memory_space=pl.ANY)
    dma = pltpu.SemaphoreType.DMA

    def v(*shape, dtype=BF):
        return pltpu.VMEM(shape, dtype)

    t, r, w, deep = t_rows, rows, width, 3 * piece + 16
    scratch = [
        v(2, 8, KP, dtype=F32), v(2, 8, KP, dtype=F32), v(ne + 8, w, dtype=F32), v(2, ne + 8, w, dtype=F32),
        v(2, w, 3 * w), v(2, w, w), v(2, w, ff), v(2, ff, w),
        v(3 * gs * TAIL, gs * MAIN),
        v(2, t, w, dtype=F32), v(2, t, 1, dtype=F32), v(2, t, w, dtype=F32), v(2, t, 1, dtype=F32),
        v(2, KP, w), v(2, KP, 3 * w), v(2, HEADS, t, KP, dtype=F32), v(2, KP, w),
        v(t, w, dtype=F32), v(2, KP, w), v(2, t, ne, dtype=F32),
        v(2, t, 8, dtype=F32), v(2, 2, t, 1, dtype=F32), v(2, 2, t, w), v(2, 2, t, r), v(2, r, 2 * KP),
        v(4, ne, 64, LANE), v(8, ne, 64, LANE), v(2, 2, r, w), v(2, 2, r, ff), v(2, 2, r, ff), v(2, 2, r, w),
        v(r, w),
        v(2, KP, w), v(t, w, dtype=F32), v(KP, w), v(KP, 3 * w), v(t, w, dtype=F32),
        v(2, t, w), v(t, w), v(2, t, w, dtype=F32), v(t, w, dtype=F32),
        v(w, ff), v(ff, w), v(w, ff), v(ff, w),
        v(2, ne, deep, LANE), v(ne, deep, LANE), v(ne, 16, LANE, dtype=F32), v(ne, deep, LANE),
        v(deep, LANE, dtype=F32), v(deep, LANE, dtype=F32), v(deep, LANE), v(ne, deep, LANE),
        v(4, w, w), v(ne, 16, LANE, dtype=F32),
        dma((2, 6)), dma((6,)), dma((4,)), dma((8, GROUPS)), dma((6,)), dma((6,)), dma((5,)), dma((5,)),
        dma, dma, dma, dma, dma, dma, dma, dma, dma((11,)),
    ]
    shapes = [
        ((seq, 2, w), BF), ((2 * seq, 1, w), F32), ((ne, w), F32), ((1, w), F32), ((1, w), F32), ((w, 3 * w), BF), ((w, w), BF),
        ((w, ff), BF), ((ff, w), BF),
    ]
    act, grad, d_router, d_gain_one, d_gain_two, d_qkv, d_out, d_in, d_back = pl.pallas_call(
        lambda *refs: kernel((seq, width, ff, ne), *refs),
        out_shape=[jax.ShapeDtypeStruct(s, d) for s, d in shapes],
        in_specs=[vmem] * 7 + [anywhere] * 4,
        out_specs=[vmem] * 5 + [anywhere] * 4,
        scratch_shapes=scratch,
        compiler_params=pltpu.CompilerParams(
            collective_id=0, has_side_effects=True, vmem_limit_bytes=62 * 2**20
        ),
        name="blocks",
    )(
        own(images_in), own(cotangent),
        jnp.swapaxes(routes[0, :, 0], 1, 2), jnp.swapaxes(keep[0, :, 0], 1, 2),
        gain_one, gain_two, w_router[0].T, w_qkv, w_out, w_in, w_back,
    )
    return (
        act.transpose(1, 0, 2)[None, :, None],
        grad.reshape(2, seq, w)[None, :, None],
        d_gain_one,
        d_qkv.astype(F32)[None],
        d_out.astype(F32)[None],
        d_gain_two,
        d_router.T[None],
        d_in.astype(F32)[None, None],
        d_back.astype(F32)[None, None],
    )


def solution(mesh):
    spread = ("expert", "dp")
    tokens = P(None, spread, None, None)
    per_block = P("section", None, spread, None, None)
    vector, matrix, experts = P("section", None), P("section", None, None), P("section", "expert", None, None)
    return jax.shard_map(
        body,
        mesh=mesh,
        in_specs=(
            tokens, tokens, vector, matrix, matrix, vector, matrix, experts, experts, per_block, per_block,
        ),
        out_specs=(
            per_block, per_block, vector, matrix, matrix, vector, matrix, experts, experts,
        ),
        check_vma=False,
    )
```

```python
import math

import jax
import jax.numpy as jnp
from jax import lax
from jax.experimental import pallas as pl
from jax.experimental.pallas import tpu as pltpu
from jax.sharding import PartitionSpec as P

HEADS = 6
HEAD = 64
PAIR = 2 * HEAD
SCALE = HEAD ** (-0.5)
EPSILON = 1e-06
HIGHEST = lax.Precision.HIGHEST
BF = jnp.bfloat16
F32 = jnp.float32
LANE = 128
MAIN = 16
TAIL = 4
KP = 256
CHUNK = 512
ORDER = (0, 1, 4, 5, 6, 7, 2, 3)
SPLIT = 7
GROUPS = 4
MESH = pl.DeviceIdType.MESH


def mm(a, b, precision=None):
    return lax.dot_general(a, b, (((1,), (0,)), ((), ())), precision=precision, preferred_element_type=F32)


def mm_nt(a, b, precision=None):
    return lax.dot_general(a, b, (((1,), (1,)), ((), ())), precision=precision, preferred_element_type=F32)


def mm_tn(a, b, precision=None):
    return lax.dot_general(a, b, (((0,), (0,)), ((), ())), precision=precision, preferred_element_type=F32)


def iota(shape, dim):
    return lax.broadcasted_iota(jnp.int32, shape, dim)


def one_hot(hit, dtype=BF):
    return jnp.where(hit, 1.0, 0.0).astype(dtype)


def phi_of(h):
    return 0.5 * lax.erf(h * (0.5**0.5)) + 0.5


def slope_of(h, phi):
    return phi + h * (jnp.exp(h * h * -0.5) * (1.0 / math.sqrt(2.0 * math.pi)))


def norm_parts(x):
    cen = x - jnp.mean(x, axis=-1, keepdims=True)
    rstd = lax.rsqrt(jnp.mean(cen * cen, axis=-1, keepdims=True) + EPSILON)
    return cen * rstd, rstd


def norm_back(d_hat, hat, rstd):
    return rstd * (
        d_hat
        - jnp.mean(d_hat, axis=-1, keepdims=True)
        - hat * jnp.mean(d_hat * hat, axis=-1, keepdims=True)
    )


def kernel(dims, *refs):
    seq, width, ff, ne = dims
    t_rows = -(-seq // 16) * 16
    gs = ne // GROUPS
    gm, gt = gs * MAIN, gs * TAIL
    gr = gm + gt
    rows = ne * (MAIN + TAIL)
    piece = width * 4 // ne
    per = ne // 4
    (
        images, cot, routes, keep, gain_one, gain_two, router, w_qkv, w_out, w_in, w_back,
        act_h, ig_h, router_h, gain1_h, gain2_h, qkv_o, out_o, wi_o, wb_o,
        meta_m, meta_s, small_m, small_s, wqkv_s, wout_s, win_s, wback_s,
        s_s, xh1, rs1, xh2, rs2, nrm, qs, ps, att, mix, sec, prb, cols_s, gate_s, pk, dd, dt,
        tx, rx, in_s, ac_s, dg_s, dp_s, ret, vs, dsr, dbr, dqkv, dmx, ya, ya_rx, gx, gx_rx,
        wtx_i, wtx_b, wrc_i, wrc_b,
        den, den_rc, smt, rs_rx, dpt, dpr, agt, ag_rx, dfin_q, smfin, act_o, ig_o, router_o, gain1_o, gain2_o,
        wsem, wsend, a2s, a2r, cxs, cxr, dps, dpr_sem, rss, rsr, ags, agr, acs, acr, igs, igr, osem,
    ) = refs
    core = lax.axis_index("section")
    me = lax.axis_index("expert")
    half = lax.axis_index("dp")
    other = 1 - core

    def expert_at(k):
        return lax.rem(me + k, ne)

    def wait(ref, sem):
        pltpu.make_async_copy(ref, ref, sem).wait()

    def to_core(src, dst, send, recv):
        return pltpu.make_async_remote_copy(
            src_ref=src, dst_ref=dst, send_sem=send, recv_sem=recv,
            device_id={"section": other}, device_id_type=MESH,
        )

    def to_dp(src, dst, send, recv):
        return pltpu.make_async_remote_copy(
            src_ref=src, dst_ref=dst, send_sem=send, recv_sem=recv,
            device_id={"dp": 1 - half}, device_id_type=MESH,
        )

    barrier = pltpu.get_barrier_semaphore()

    def greet(k, _):
        pl.semaphore_signal(barrier, inc=1, device_id={"expert": expert_at(k)}, device_id_type=MESH)
        return _

    pl.semaphore_signal(barrier, inc=1, device_id={"section": other}, device_id_type=MESH)
    pl.semaphore_signal(barrier, inc=1, device_id={"dp": 1 - half}, device_id_type=MESH)
    lax.fori_loop(1, ne, greet, 0)

    which = iota((8, KP), 0)
    for m in range(2):
        meta_m[m] = jnp.where(which < 2, -64.0, 0.0)
        meta_m[m, 0:2, 0:seq] = routes[m].astype(F32)
        meta_m[m, 2:4, 0:seq] = keep[m].astype(F32)
    small_m[0:ne] = router[...]
    small_m[ne:ne + 1] = gain_one[...]
    small_m[ne + 1:ne + 2] = gain_two[...]
    small_m[ne + 2:ne + 8] = jnp.zeros((6, width), F32)
    held = [
        (meta_m.at[core], meta_m.at[other], meta_s),
        (small_m, small_m, small_s),
        (w_qkv.at[0], w_qkv.at[0], wqkv_s),
        (w_out.at[0], w_out.at[0], wout_s),
        (w_in.at[0, 0], w_in.at[0, 0], win_s),
        (w_back.at[0, 0], w_back.at[0, 0], wback_s),
    ]
    for i, (mine, _, dst) in enumerate(held):
        pltpu.make_async_copy(mine, dst.at[core], wsem.at[core, i]).start()

    for ref in (nrm, qs, att, sec):
        for b in range(2):
            ref[b, t_rows:KP, :] = jnp.zeros((KP - t_rows, ref.shape[2]), BF)
    for ref in (dbr, dqkv):
        ref[t_rows:KP, :] = jnp.zeros((KP - t_rows, ref.shape[1]), BF)
    for b in range(2):
        vs[b, t_rows:KP, :] = jnp.zeros((KP - t_rows, width), BF)
    smt[...] = jnp.zeros(smt.shape, F32)
    row, col = iota((3 * gt, gm), 0), iota((3 * gt, gm), 1)
    chunk = (row >= gt).astype(jnp.int32) + (row >= 2 * gt).astype(jnp.int32)
    n = row - chunk * gt
    bits = gs.bit_length() - 1
    s_s[...] = one_hot(((col >> 4) == (n & (gs - 1))) & ((col & 15) == 4 * chunk + (n >> bits)))

    pl.semaphore_wait(barrier, ne + 1)
    for i, (_, theirs, dst) in enumerate(held):
        to_core(theirs, dst.at[core], wsend.at[i], wsem.at[core, i]).start()

    def weight(b, i):
        wait(held[i][2].at[b], wsem.at[b, i])

    def send(phase, g, rows_of, back):
        main, tail = rows_of[0:gm], rows_of[gm:gr]
        at = pl.ds(g * gs, gs)
        slot = ORDER.index(phase) % 4
        if g == (GROUPS - 1 if back else 0) and ORDER.index(phase) >= 4:
            wait(tx.at[slot, pl.ds(1, ne - 1)], a2s.at[slot])
        for c in range(3):
            tx[slot, at, 16 * c:16 * c + 16, :] = main[:, LANE * c:LANE * c + LANE].reshape(gs, 16, LANE)
        stack = jnp.concatenate([tail[:, LANE * c:LANE * c + LANE] for c in range(3)], axis=0)
        tx[slot, at, 48:64, :] = mm_tn(s_s[...], stack).astype(BF).reshape(gs, 16, LANE)
        own = 0 if back else ne - 1
        first = 1 if back and g == 0 else g * gs
        last = ne - 1 if not back and g == GROUPS - 1 else g * gs + gs

        def step(i, _):
            pltpu.make_async_remote_copy(
                src_ref=tx.at[slot, i], dst_ref=rx.at[phase, ne - 1 - i],
                send_sem=a2s.at[slot], recv_sem=a2r.at[phase, GROUPS - 1 - g],
                device_id={"expert": expert_at(i if back else i + 1)}, device_id_type=MESH,
            ).start()
            return _

        lax.fori_loop(first, last, step, 0)
        if g * gs <= own < g * gs + gs:
            pltpu.make_async_copy(
                tx.at[slot, own], rx.at[phase, ne - 1 - own], a2r.at[phase, GROUPS - 1 - g]
            ).start()

    def receive(phase, g, out, start):
        at = pl.ds(g * gs, gs)
        wait(rx.at[phase, at], a2r.at[phase, g])
        for c in range(3):
            out[start:start + gm, LANE * c:LANE * c + LANE] = rx[phase, at, 16 * c:16 * c + 16, :].reshape(gm, LANE)
        tail = mm(s_s[...], rx[phase, at, 48:64, :].reshape(gm, LANE)).astype(BF)
        for c in range(3):
            out[start + gm:start + gr, LANE * c:LANE * c + LANE] = tail[c * gt:c * gt + gt]

    def place_of(rank, slot):
        group = jnp.floor(rank * (1.0 / gs))
        within = rank - group * gs
        return group * gr + jnp.where(slot < MAIN, within * MAIN + slot, gm + (slot - MAIN) * gs + within)

    def route(b):
        data = meta_s[b]
        mef = (me + 1).astype(F32)
        chosen, keeps = [data[0:1], data[1:2]], [data[2:3], data[3:4]]
        rank = [r - mef for r in chosen]
        rank = [jnp.where(r < 0.0, r + ne, r) for r in rank]
        lanes = iota((ne, KP), 0).astype(F32)
        marks = [one_hot(lanes == r, F32) for r in rank]
        earlier = one_hot(iota((KP, KP), 0) < iota((KP, KP), 1))
        before = mm((marks[0] + marks[1]).astype(BF), earlier)
        slot = [jnp.sum(before * m, axis=0, keepdims=True) for m in marks]
        spot = iota((rows, KP), 0).astype(F32)
        for k in range(2):
            dt[b, :, KP * k:KP * k + KP] = one_hot(spot == place_of(rank[k], slot[k]))
        which = iota((8, KP), 0)
        lines = jnp.zeros((8, KP), F32)
        for i, line in enumerate((*rank, *slot, *keeps, *chosen)):
            lines = jnp.where(which == i, line, lines)
        same = one_hot(iota((t_rows, KP), 0) == iota((t_rows, KP), 1))
        cols = mm_nt(same, lines.astype(BF))
        cols_s[b] = cols
        spot = iota((t_rows, rows), 1).astype(F32)
        for k in range(2):
            dd[b, k] = one_hot(spot == place_of(cols[:, k:k + 1], cols[:, 2 + k:3 + k]))

    def chosen_marks(b):
        lanes = iota((t_rows, ne), 1).astype(F32)
        return [one_hot(lanes == cols_s[b, :, 6 + k:7 + k], F32) * cols_s[b, :, 4 + k:5 + k] for k in range(2)]

    def head_masks():
        lanes = iota((1, PAIR), 1)
        return [one_hot(lanes < HEAD), one_hot(lanes >= HEAD)]

    def forward_dense(b, x):
        hat, rstd = norm_parts(x)
        xh1[b], rs1[b] = hat, rstd
        normed = (hat * small_s[b, ne:ne + 1, :]).astype(BF)
        nrm[b, 0:t_rows, :] = normed
        weight(b, 2)
        qs[b, 0:t_rows, :] = mm(normed, wqkv_s[b]).astype(BF)
        masks = head_masks()
        real = iota((t_rows, KP), 1) < seq
        for p in range(HEADS // 2):
            at = PAIR * p
            query, key = qs[b, 0:t_rows, at:at + PAIR], qs[b, :, width + at:width + at + PAIR]
            value = qs[b, :, 2 * width + at:2 * width + at + PAIR]
            out = jnp.zeros((t_rows, PAIR), F32)
            for h in range(2):
                scores = mm_nt(query * masks[h], key) * SCALE
                scores = jnp.where(real, scores, -1e30)
                e = jnp.exp(scores - jnp.max(scores, axis=-1, keepdims=True))
                probs = e * (1.0 / jnp.sum(e, axis=-1, keepdims=True))
                ps[b, 2 * p + h] = probs
                out = out + mm(probs.astype(BF), value * masks[h])
            att[b, 0:t_rows, at:at + PAIR] = out.astype(BF)
        weight(b, 3)
        mixed = x + mm(att[b, 0:t_rows, :], wout_s[b])
        mix[...] = mixed
        hat, rstd = norm_parts(mixed)
        xh2[b], rs2[b] = hat, rstd
        second = hat * small_s[b, ne + 1:ne + 2, :]
        sec[b, 0:t_rows, :] = second.astype(BF)
        for g in range(GROUPS):
            at = slice(g * gr, g * gr + gr)
            send(4 * b, g, mm(dt[b, at, 0:KP] + dt[b, at, KP:2 * KP], sec[b]).astype(BF), False)
        logits = mm_nt(second, small_s[b, 0:ne, :], HIGHEST)
        e = jnp.exp(logits - jnp.max(logits, axis=-1, keepdims=True))
        probs = e / jnp.sum(e, axis=-1, keepdims=True)
        prb[b] = probs
        for k, marks in enumerate(chosen_marks(b)):
            gate_s[b, k] = jnp.sum(marks * probs, axis=-1, keepdims=True)

    steps = ff // CHUNK

    def chunk_at(i):
        return pl.ds(pl.multiple_of(i * CHUNK, CHUNK), CHUNK)

    def forward_expert(b):
        weight(b, 4)
        weight(b, 5)
        for h in range(GROUPS - 1, -1, -1):
            at = slice(h * gr, h * gr + gr)
            receive(4 * b, h, in_s.at[b, 0], h * gr)
            hidden = mm(in_s[b, 0, at, :], win_s[b])
            active = (hidden * phi_of(hidden)).astype(BF)
            ac_s[b, 0, at, :] = active
            send(4 * b + 1, h, mm(active, wback_s[b]).astype(BF), True)

    def slopes(b, side):
        def step(i, _):
            cols = chunk_at(i)
            hidden = mm(in_s[b, side], win_s[b, :, cols])
            phi = phi_of(hidden)
            dg_s[b, side, :, cols] = slope_of(hidden, phi).astype(BF)
            if side == 1:
                ac_s[b, side, :, cols] = (hidden * phi).astype(BF)
            return _

        lax.fori_loop(0, steps, step, 0)

    def rows_to_dp(ref, b, i, low, high):
        at = pl.ds(low * (rows // 10), (high - low) * (rows // 10))
        to_dp(ref.at[b, 0, at], ref.at[b, 1, at], dps.at[i], dpr_sem.at[i]).start()

    def rows_from_dp(ref, b, i):
        wait(ref.at[b, 1], dpr_sem.at[i])

    def forward_combine(b):
        for g in range(GROUPS):
            receive(4 * b + 1, g, ret, g * gr)
        y = mix[...]
        for k in range(2):
            picked = mm(dd[b, k], ret[...])
            pk[b, k] = picked.astype(BF)
            y = y + gate_s[b, k] * picked
        low = y.astype(BF)
        ya[b] = low
        return low.astype(F32)

    def backward_start(b, dy):
        d_probs = jnp.zeros((t_rows, ne), F32)
        for k, marks in enumerate(chosen_marks(b)):
            d_gate = jnp.sum(dy * pk[b, k].astype(F32), axis=-1, keepdims=True)
            d_probs = d_probs + marks * d_gate
            vs[k, 0:t_rows, :] = (gate_s[b, k] * dy).astype(BF)
        for g in range(GROUPS):
            at = slice(g * gr, g * gr + gr)
            part = mm(dt[b, at, 0:KP], vs[0]) + mm(dt[b, at, KP:2 * KP], vs[1])
            send(4 * b + 2, g, part.astype(BF), False)
        probs = prb[b]
        d_logits = probs * (d_probs - jnp.sum(probs * d_probs, axis=-1, keepdims=True))
        dsr[...] = mm(d_logits, small_s[b, 0:ne, :], HIGHEST)
        return mm_tn(d_logits, xh2[b] * small_s[b, ne + 1:ne + 2, :], HIGHEST)

    def hidden_grad(b, side, at, cols):
        slope = dg_s[b, side, at, cols].astype(F32)
        d_hidden = (mm_nt(dp_s[b, side, at, :], wback_s[b, cols, :]) * slope).astype(BF)
        dg_s[b, side, at, cols] = d_hidden
        return d_hidden

    def backward_expert(b):
        for h in range(GROUPS - 1, -1, -1):
            at = slice(h * gr, h * gr + gr)
            receive(4 * b + 2, h, dp_s.at[b, 0], h * gr)
            d_hidden = hidden_grad(b, 0, at, slice(None))
            send(4 * b + 3, h, mm_nt(d_hidden, win_s[b]).astype(BF), True)

    def far_hidden_grad(b):
        rows_from_dp(dp_s, b, 2 + b)

        def step(i, _):
            hidden_grad(b, 1, slice(None), chunk_at(i))
            return _

        lax.fori_loop(0, steps, step, 0)

    def in_grads(b):
        def step(i, _):
            cols = chunk_at(i)
            grad = mm_tn(in_s[b].reshape(2 * rows, width), dg_s[b, :, :, cols].reshape(2 * rows, CHUNK))
            wtx_i[:, cols] = grad.astype(BF)
            return _

        lax.fori_loop(0, steps, step, 0)

        @pl.when(core != b)
        def _():
            to_core(wtx_i, wrc_i, cxs.at[0], cxr.at[0]).start()

    def back_grads(b):
        def step(i, _):
            cols = chunk_at(i)
            grad = mm_tn(ac_s[b, :, :, cols].reshape(2 * rows, CHUNK), dp_s[b].reshape(2 * rows, width))
            wtx_b[cols, :] = grad.astype(BF)
            return _

        lax.fori_loop(0, steps, step, 0)

        @pl.when(core != b)
        def _():
            to_core(wtx_b, wrc_b, cxs.at[1], cxr.at[1]).start()

    def expert_out(b):
        @pl.when(core == b)
        def _():
            wait(wrc_i, cxr.at[0])
            wtx_i[...] = (wtx_i[...].astype(F32) + wrc_i[...].astype(F32)).astype(BF)
            pltpu.make_async_copy(wtx_i, wi_o, osem.at[0]).start()
            wait(wrc_b, cxr.at[1])
            wtx_b[...] = (wtx_b[...].astype(F32) + wrc_b[...].astype(F32)).astype(BF)
            pltpu.make_async_copy(wtx_b, wb_o, osem.at[1]).start()

    def in_sent(b):
        @pl.when(core != b)
        def _():
            wait(wtx_i, cxs.at[0])

        @pl.when(core == b)
        def _():
            wait(wi_o, osem.at[0])

    def back_sent(b):
        @pl.when(core != b)
        def _():
            wait(wtx_b, cxs.at[1])

        @pl.when(core == b)
        def _():
            wait(wb_o, osem.at[1])

    def dense_part(b, q, grad, smalls=()):
        at = slice(q * per, q * per + per)
        for c in range(3):
            part = grad[:, LANE * c:LANE * c + LANE].astype(BF)
            den[b, at, piece * c:piece * c + piece, :] = part.reshape(per, piece, LANE)
        for first, small in smalls:
            for c in range(3):
                smt[0, first + c:first + c + 1, :] = small[:, LANE * c:LANE * c + LANE]
        den[b, at, 3 * piece:3 * piece + 16, :] = smt[at].astype(BF)

        @pl.when(core != b)
        def _():
            to_core(den.at[b, at], den_rc.at[at], cxs.at[2 + q], cxr.at[2 + q]).start()

    def dense_out(b, d_router):
        for c in range(3):
            smt[:, c, :] = d_router[:, LANE * c:LANE * c + LANE]
        dense_part(b, 3, mm_tn(att[b], dbr[...]))

    def dense_qkv(b, q, smalls=()):
        dense_part(b, q, mm_tn(nrm[b], dqkv[:, width * q:width * q + width]), smalls)

    def dense_sent(b):
        @pl.when(core != b)
        def _():
            for q in range(4):
                at = slice(q * per, q * per + per)
                wait(den.at[b, at], cxs.at[2 + q])

        @pl.when(core == b)
        def _():
            wait(den.at[b, pl.ds(1, ne - 1)], rss)

    def backward_attention(b, dy, early=None):
        for g in range(GROUPS):
            receive(4 * b + 3, g, ret, g * gr)
        d_second = mm(dd[b, 0] + dd[b, 1], ret[...]) + dsr[...]
        hat2 = xh2[b]
        d_gain_two = jnp.sum(d_second * hat2, axis=0, keepdims=True)
        d_mixed = dy + norm_back(d_second * small_s[b, ne + 1:ne + 2, :], hat2, rs2[b])
        dmx[...] = d_mixed
        d_branch = d_mixed.astype(BF)
        dbr[0:t_rows, :] = d_branch
        d_att = mm_nt(d_branch, wout_s[b]).astype(BF)
        if early is not None:
            early()
        masks = head_masks()
        for p in range(HEADS // 2):
            at = PAIR * p
            query, key = qs[b, 0:t_rows, at:at + PAIR], qs[b, :, width + at:width + at + PAIR]
            value = qs[b, :, 2 * width + at:2 * width + at + PAIR]
            d_query = jnp.zeros((t_rows, PAIR), F32)
            d_key = jnp.zeros((KP, PAIR), F32)
            d_value = jnp.zeros((KP, PAIR), F32)
            for h in range(2):
                d_out = d_att[:, at:at + PAIR] * masks[h]
                probs = ps[b, 2 * p + h]
                d_value = d_value + mm_tn(probs.astype(BF), d_out)
                d_probs = mm_nt(d_out, value)
                inner = jnp.sum(probs * d_probs, axis=-1, keepdims=True)
                d_scores = (probs * (d_probs - inner)).astype(BF)
                d_query = d_query + mm(d_scores, key * masks[h])
                d_key = d_key + mm_tn(d_scores, query * masks[h])
            dqkv[0:t_rows, at:at + PAIR] = (d_query * SCALE).astype(BF)
            dqkv[:, width + at:width + at + PAIR] = (d_key * SCALE).astype(BF)
            dqkv[:, 2 * width + at:2 * width + at + PAIR] = d_value.astype(BF)
        return d_gain_two

    def backward_input(b):
        d_normed = mm_nt(dqkv[0:t_rows, :], wqkv_s[b])
        hat1 = xh1[b]
        d_gain_one = jnp.sum(d_normed * hat1, axis=0, keepdims=True)
        return dmx[...] + norm_back(d_normed * small_s[b, ne:ne + 1, :], hat1, rs1[b]), d_gain_one

    def dense_scatter(b, q):
        @pl.when(core == b)
        def _():
            at = slice(q * per, q * per + per)
            wait(den_rc.at[at], cxr.at[2 + q])

            den[b, at] = (den[b, at].astype(F32) + den_rc[at].astype(F32)).astype(BF)

            def step(to, carry):
                @pl.when(to != me)
                def _():
                    pltpu.make_async_remote_copy(
                        src_ref=den.at[b, to], dst_ref=rs_rx.at[lax.rem(me - to + ne, ne)], send_sem=rss, recv_sem=rsr,
                        device_id={"expert": to}, device_id_type=MESH,
                    ).start()

                return carry

            lax.fori_loop(q * per, q * per + per, step, 0)

    def dense_reduce(b):
        @pl.when(core == b)
        def _():
            wait(rs_rx.at[pl.ds(1, ne - 1)], rsr)

            def step(k, total):
                return total + rs_rx[k].astype(F32)

            dpt[...] = lax.fori_loop(1, ne, step, den[b, me].astype(F32))
            to_dp(dpt, dpr, dps.at[4], dpr_sem.at[4]).start()

    def dense_gather(b):
        @pl.when(core == b)
        def _():
            wait(dpr, dpr_sem.at[4])
            agt[...] = (dpt[...] + dpr[...]).astype(BF)

            def step(k, _):
                to = expert_at(k)
                pltpu.make_async_remote_copy(
                    src_ref=agt, dst_ref=ag_rx.at[ne - k], send_sem=ags, recv_sem=agr,
                    device_id={"expert": to}, device_id_type=MESH,
                ).start()
                return _

            lax.fori_loop(1, ne, step, 0)

    def dense_finish(b):
        @pl.when(core == b)
        def _():
            wait(ag_rx.at[pl.ds(1, ne - 1)], agr)
            ag_rx[0] = agt[...]

            def step(k, _):
                to = expert_at(k)
                smfin[to] = ag_rx[k, 3 * piece:3 * piece + 16, :].astype(F32)
                block, at = lax.div(to, per), pl.multiple_of(lax.rem(to, per) * piece, 16)
                for c in range(3):
                    dfin_q[block, pl.ds(at, piece), LANE * c:LANE * c + LANE] = ag_rx[k, piece * c:piece * c + piece, :]
                return _

            lax.fori_loop(0, ne, step, 0)
            for q in range(3):
                pltpu.make_async_copy(dfin_q.at[q], qkv_o.at[:, pl.ds(width * q, width)], osem.at[6 + q]).start()
            pltpu.make_async_copy(dfin_q.at[3], out_o, osem.at[9]).start()
            for c in range(3):
                at = slice(LANE * c, LANE * c + LANE)
                router_o[:, at] = smfin[:, c, :]
                gain1_o[:, at] = smfin[0, 3 + c:4 + c, :]
                gain2_o[:, at] = smfin[0, 6 + c:7 + c, :]
            wait(ag_rx.at[pl.ds(1, ne - 1)], ags)
            wait(dpt, dps.at[4])

    x = images[...].astype(F32)
    weight(0, 0)
    weight(0, 1)
    route(0)
    forward_dense(0, x)
    weight(1, 0)
    weight(1, 1)
    route(1)
    forward_expert(0)
    rows_to_dp(in_s, 0, 0, 0, SPLIT)
    slopes(0, 0)
    x = forward_combine(0)
    forward_dense(1, x)
    rows_to_dp(in_s, 0, 0, SPLIT, 10)
    forward_expert(1)
    rows_to_dp(in_s, 1, 1, 0, SPLIT)
    slopes(1, 0)
    forward_combine(1)
    dy = cot[...].astype(F32)
    d_router = backward_start(1, dy)
    rows_to_dp(in_s, 1, 1, SPLIT, 10)
    to_core(ya.at[other], ya_rx, acs, acr).start()
    rows_from_dp(in_s, 0, 0)
    slopes(0, 1)
    backward_expert(1)
    rows_to_dp(dp_s, 1, 3, 0, SPLIT)
    rows_from_dp(in_s, 1, 1)
    slopes(1, 1)
    d_gain_two = backward_attention(1, dy)
    dx, d_gain_one = backward_input(1)
    dy = dx.astype(BF).astype(F32)
    gx[1] = dy
    d_router_0 = backward_start(0, dy)
    rows_to_dp(dp_s, 1, 3, SPLIT, 10)
    dense_out(1, d_router)
    dense_qkv(1, 2)
    dense_qkv(1, 1)
    dense_qkv(1, 0, ((3, d_gain_one), (6, d_gain_two)))
    backward_expert(0)
    for q in (3, 2, 1, 0):
        dense_scatter(1, q)
    rows_to_dp(dp_s, 0, 2, 0, 10)
    far_hidden_grad(1)
    in_grads(1)
    back_grads(1)
    d_gain_two = backward_attention(0, dy, lambda: dense_out(0, d_router_0))
    dense_qkv(0, 2)
    dense_scatter(0, 3)
    dense_qkv(0, 1)
    dx, d_gain_one = backward_input(0)
    dense_qkv(0, 0, ((3, d_gain_one), (6, d_gain_two)))
    dense_reduce(1)
    dense_scatter(0, 2)
    dense_scatter(0, 1)
    dense_scatter(0, 0)
    gx[0] = dx
    to_core(gx.at[other], gx_rx, igs, igr).start()
    expert_out(1)
    dense_gather(1)
    far_hidden_grad(0)
    in_sent(1)
    in_grads(0)
    dense_reduce(0)
    dense_gather(0)
    back_sent(1)
    back_grads(0)
    dense_finish(1)
    wait(ya_rx, acr)
    mine, theirs = ya[core].astype(F32), ya_rx[...].astype(F32)
    pair = [jnp.where(core == m, mine, theirs)[0:seq] for m in range(2)]
    act_o[...] = jnp.concatenate([p.reshape(seq, 1, width) for p in pair], axis=1).astype(BF)
    wait(gx_rx, igr)
    ig_o[pl.ds(core * seq, seq), 0, :] = gx[core, 0:seq, :]
    ig_o[pl.ds(other * seq, seq), 0, :] = gx_rx[0:seq, :]
    pltpu.make_async_copy(act_o, act_h, osem.at[2]).start()
    pltpu.make_async_copy(ig_o, ig_h, osem.at[3]).start()
    expert_out(0)
    dense_finish(0)
    smalls = ((router_o, router_h), (gain1_o, gain1_h), (gain2_o, gain2_h))
    for i, (source, out) in enumerate(smalls):
        pltpu.make_async_copy(source, out, osem.at[(4, 5, 10)[i]]).start()
    in_sent(0)
    back_sent(0)
    dense_sent(0)
    dense_sent(1)
    for i, (_, theirs, _dst) in enumerate(held):
        wait(theirs, wsend.at[i])
    for slot in range(4):
        wait(tx.at[slot, pl.ds(1, ne - 1)], a2s.at[slot])
    for b in range(2):
        wait(in_s.at[b, 0], dps.at[b])
        wait(dp_s.at[b, 0], dps.at[2 + b])
    wait(ya.at[other], acs)
    wait(gx.at[other], igs)
    for q in range(3):
        wait(dfin_q.at[q], osem.at[6 + q])
    wait(out_o, osem.at[9])
    wait(act_h, osem.at[2])
    wait(ig_h, osem.at[3])
    for i, (_, out) in enumerate(smalls):
        wait(out, osem.at[(4, 5, 10)[i]])


def body(images_in, cotangent, gain_one, w_qkv, w_out, gain_two, w_router, w_in, w_back, routes, keep):
    micro, _, seq, width = images_in.shape
    ne = lax.axis_size("expert")
    ff = w_in.shape[3]
    t_rows = -(-seq // 16) * 16
    rows = ne * (MAIN + TAIL)
    gs = ne // GROUPS
    piece = 4 * width // ne
    core = lax.axis_index("section")

    def own(tokens):
        mine = lax.dynamic_index_in_dim(tokens[:, 0], core, 0, keepdims=False)
        return jnp.pad(mine, ((0, t_rows - seq), (0, 0)))

    vmem, anywhere = pl.BlockSpec(memory_space=pltpu.VMEM), pl.BlockSpec(memory_space=pl.ANY)
    dma = pltpu.SemaphoreType.DMA

    def v(*shape, dtype=BF):
        return pltpu.VMEM(shape, dtype)

    t, r, w, deep = t_rows, rows, width, 3 * piece + 16
    scratch = [
        v(2, 8, KP, dtype=F32), v(2, 8, KP, dtype=F32), v(ne + 8, w, dtype=F32), v(2, ne + 8, w, dtype=F32),
        v(2, w, 3 * w), v(2, w, w), v(2, w, ff), v(2, ff, w),
        v(3 * gs * TAIL, gs * MAIN),
        v(2, t, w, dtype=F32), v(2, t, 1, dtype=F32), v(2, t, w, dtype=F32), v(2, t, 1, dtype=F32),
        v(2, KP, w), v(2, KP, 3 * w), v(2, HEADS, t, KP, dtype=F32), v(2, KP, w),
        v(t, w, dtype=F32), v(2, KP, w), v(2, t, ne, dtype=F32),
        v(2, t, 8, dtype=F32), v(2, 2, t, 1, dtype=F32), v(2, 2, t, w), v(2, 2, t, r), v(2, r, 2 * KP),
        v(4, ne, 64, LANE), v(8, ne, 64, LANE), v(2, 2, r, w), v(2, 2, r, ff), v(2, 2, r, ff), v(2, 2, r, w),
        v(r, w),
        v(2, KP, w), v(t, w, dtype=F32), v(KP, w), v(KP, 3 * w), v(t, w, dtype=F32),
        v(2, t, w), v(t, w), v(2, t, w, dtype=F32), v(t, w, dtype=F32),
        v(w, ff), v(ff, w), v(w, ff), v(ff, w),
        v(2, ne, deep, LANE), v(ne, deep, LANE), v(ne, 16, LANE, dtype=F32), v(ne, deep, LANE),
        v(deep, LANE, dtype=F32), v(deep, LANE, dtype=F32), v(deep, LANE), v(ne, deep, LANE),
        v(4, w, w), v(ne, 16, LANE, dtype=F32),
        v(seq, 2, w), v(2 * seq, 1, w, dtype=F32), v(ne, w, dtype=F32), v(1, w, dtype=F32), v(1, w, dtype=F32),
        dma((2, 6)), dma((6,)), dma((4,)), dma((8, GROUPS)), dma((6,)), dma((6,)), dma((5,)), dma((5,)),
        dma, dma, dma, dma, dma, dma, dma, dma, dma((11,)),
    ]
    shapes = [
        ((seq, 2, w), BF), ((2 * seq, 1, w), F32), ((ne, w), F32), ((1, w), F32), ((1, w), F32), ((w, 3 * w), BF), ((w, w), BF),
        ((w, ff), BF), ((ff, w), BF),
    ]
    act, grad, d_router, d_gain_one, d_gain_two, d_qkv, d_out, d_in, d_back = pl.pallas_call(
        lambda *refs: kernel((seq, width, ff, ne), *refs),
        out_shape=[jax.ShapeDtypeStruct(s, d) for s, d in shapes],
        in_specs=[vmem] * 7 + [anywhere] * 4,
        out_specs=[anywhere] * 9,
        scratch_shapes=scratch,
        compiler_params=pltpu.CompilerParams(
            collective_id=0, has_side_effects=True, vmem_limit_bytes=62 * 2**20
        ),
        name="blocks",
    )(
        own(images_in), own(cotangent),
        jnp.swapaxes(routes[0, :, 0], 1, 2), jnp.swapaxes(keep[0, :, 0], 1, 2),
        gain_one, gain_two, w_router[0].T, w_qkv, w_out, w_in, w_back,
    )
    return (
        act.transpose(1, 0, 2)[None, :, None],
        grad.reshape(2, seq, w)[None, :, None],
        d_gain_one,
        d_qkv.astype(F32)[None],
        d_out.astype(F32)[None],
        d_gain_two,
        d_router.T[None],
        d_in.astype(F32)[None, None],
        d_back.astype(F32)[None, None],
    )


def solution(mesh):
    spread = ("expert", "dp")
    tokens = P(None, spread, None, None)
    per_block = P("section", None, spread, None, None)
    vector, matrix, experts = P("section", None), P("section", None, None), P("section", "expert", None, None)
    return jax.shard_map(
        body,
        mesh=mesh,
        in_specs=(
            tokens, tokens, vector, matrix, matrix, vector, matrix, experts, experts, per_block, per_block,
        ),
        out_specs=(
            per_block, per_block, vector, matrix, matrix, vector, matrix, experts, experts,
        ),
        check_vma=False,
    )
```
